128 devices in a mesh: cube: 8 (over z, x_lo), blk: 16 (over y, x_hi, core).
Axes of the slice: x: 4 (x_hi: 2, x_lo: 2; x = x_hi * 2 + x_lo), y: 4, z: 4, core: 2. Of those that a mesh axis runs over, the one named last changes fastest.
Arguments:
- rows: bfloat16 [196608, 1024], P(('cube', 'blk')), may hold values from -10 to 10
- start_vec: float32 [1024], replicated, may hold values from -6 to 6
- leave: int32 [2, 196608], P(None, ('cube', 'blk')), may hold values from 0 to 1, as said below
- owner: int32 [196608, 1], P(('cube', 'blk')), may hold values from 0 to 15; in each aligned block of 1536 rows (0 to 1535, 1536 to 3071, ...) at most 192 rows name the same one
Outputs:
- scores: float32 [2, 196608], P(None, ('cube', 'blk'))
- leaf_rows: bfloat16 [393216, 1024], P(('cube', 'blk'))
The draws below stay inside these ranges and needn't reach their ends.
Inputs may be any that keep to these rules, and one draw needn't show every extreme that they name: `leave`: at each level a device marks exactly as many rows as the device with the same blk index whose cube index differs in bit l; at most 768 rows of one device are marked, and some device marks 768 at every level. Among the 1536 rows of one device at most 192 name one owner; some owner is named by 192 rows.
All inputs are finite; a program needn't handle non-finite values.
Results may differ from the reference program's by a relative error of at most 0.001.
Values may be sent and summed in bfloat16 or wider, within the bound.
No kernel may reach another device: no remote copies, remote signals or barrier semaphores. Data moves between devices by JAX's collectives and lax.ppermute only.
A program may use at most 128 MiB of HBM per device.

```python
import math
from functools import partial
import jax
import jax.numpy as jnp
import numpy as np
from jax import lax

D = 1024
ROWS_DEV = 1536
LEVELS = 2
ITERS = 8
CAP = 768
CAPP = 192
TOKENS = 196608
N_CUBE = 8
N_BLK = 16


def draw_rows(key, part):
    key = jax.random.fold_in(key, 5)
    key_dir, key_spread, key_noise = jax.random.split(key, 3)
    direction = jnp.clip(jax.random.normal(key_dir, (D,), jnp.float32), -4.0, 4.0) * D ** (-0.5)
    spread = jnp.clip(jax.random.normal(key_spread, (TOKENS, 1), jnp.float32), -4.0, 4.0)
    device_ids = (jnp.arange(TOKENS, dtype=jnp.int32) // ROWS_DEV).astype(jnp.float32)
    frac = device_ids / max(TOKENS // ROWS_DEV - 1, 1)
    noise = jnp.clip(jax.random.normal(key_noise, (TOKENS, D), jnp.float32), -5.0, 5.0)
    level = 1.0 + 2.0 * frac
    drawn = noise + (spread + level[:, None]) * direction[None, :]
    return jnp.clip(drawn, -10.0, 10.0).astype(jnp.bfloat16)


def draw_leave(key, part):
    levels_out = []
    for tree_level in range(LEVELS):
        key_count, key_perm = jax.random.split(jax.random.fold_in(key, 17 + tree_level))
        drawn = jax.random.randint(key_count, (N_CUBE, N_BLK), CAP // 4, CAP + 1)
        cube_ids = jnp.arange(N_CUBE, dtype=jnp.int32)
        pair_low = cube_ids - jnp.bitwise_and(jnp.right_shift(cube_ids, tree_level), 1) * (1 << tree_level)
        counts = drawn[pair_low]
        blk_ids = jnp.arange(N_BLK, dtype=jnp.int32)
        counts = jnp.where((pair_low[:, None] == 0) & (blk_ids[None, :] == 0), CAP, counts)
        keys_all = jax.random.split(key_perm, N_CUBE * N_BLK)
        shuffled = jax.vmap(lambda one_key: jax.random.permutation(one_key, ROWS_DEV))(keys_all)
        shuffled = shuffled.reshape(N_CUBE, N_BLK, ROWS_DEV)
        levels_out.append((shuffled < counts[:, :, None]).astype(jnp.int32).reshape(-1))
    return jnp.stack(levels_out)


def shared_out(stream_key, own, number, rows, count, top, bound, skew):
    ranking = jax.random.permutation(stream_key, count)
    crowded, ordinary = load_shares(count, rows * top, bound, skew, True), load_shares(count, rows * top, bound, skew, False)
    places = jnp.arange(count)

    def named(tallies, turn):
        used = int((tallies > 0).sum())
        fixed = max(1, used // 4)
        shifted = fixed + (places - fixed + turn * (used - fixed)) % max(1, count - fixed)
        return jnp.zeros((count,), jnp.int32).at[ranking[jnp.where(places < fixed, places, shifted)]].set(jnp.asarray(tallies, jnp.int32))

    tallies = jnp.where(number % 4 == 0, named(crowded, number // 4), named(ordinary, number - number // 4 - 1))
    mixed = jax.random.permutation(jax.random.fold_in(own, 3), count)
    donor, taker = mixed[0:count // 2 * 2:2], mixed[1:count // 2 * 2:2]
    room = jnp.minimum(tallies[donor] - 1, bound - tallies[taker]) // 2
    room = jnp.where((donor == ranking[0]) | (taker == ranking[0]) | (tallies[taker] == 0), 0, jnp.maximum(room, 0))
    shifted = jax.random.randint(jax.random.fold_in(own, 4), (count // 2,), 0, 1 << 20) % (room + 1)
    tallies = tallies.at[donor].add(-shifted).at[taker].add(shifted)
    items = jnp.searchsorted(jnp.cumsum(tallies), jnp.arange(rows * top), side="right").astype(jnp.int32)
    grid = items.reshape(top, rows).T
    grid = grid[jax.random.permutation(jax.random.fold_in(own, 1), rows)]
    turn = jax.random.randint(jax.random.fold_in(own, 2), (rows, 1), 0, top)
    return jnp.take_along_axis(grid, (jnp.arange(top)[None, :] + turn) % top, axis=1)


def load_shares(count, total, bound, lean, full):
    loads = [(1 << 20) // math.isqrt(grade ** lean) + 1 for grade in range(1, count + 1)]
    largest = bound if full else min(bound, max(-(-total // count), total * loads[0] // sum(loads)))
    least = 1 if total - largest >= count - 1 else 0
    holding, spare = [largest] + [least] * (count - 1), total - largest - least * (count - 1)
    while spare > 0:
        movable = [i for i in range(1, count) if holding[i] < largest] or [i for i in range(1, count) if holding[i] < bound]
        whole, remaining = sum([loads[i] for i in movable]), spare
        for i in movable:
            more = min(bound - holding[i], max(1, remaining * loads[i] // whole), spare)
            holding[i] = holding[i] + more
            spare = spare - more
    return np.array(holding)


def bell_draw(key, dims, scale, bound, kind=jnp.bfloat16):
    return jnp.clip(scale * jax.random.normal(key, dims, jnp.float32), -bound, bound).astype(kind)


def setup_inputs(seed: int = 0) -> dict:
    streams_of = jax.random.split(jax.random.key(seed), 5)
    rows = draw_rows(jax.random.fold_in(streams_of[4], 71), 0)
    start_vec = bell_draw(streams_of[1], (D,), 1.0, 6.0, jnp.float32)
    leave = draw_leave(jax.random.fold_in(streams_of[4], 71), 0)
    owner_keys = jax.random.split(jax.random.fold_in(streams_of[3], 1), TOKENS // ROWS_DEV)
    owner_turns = jax.random.permutation(jax.random.fold_in(streams_of[3], 3), TOKENS // ROWS_DEV)
    owner = jax.vmap(lambda own, number: shared_out(jax.random.fold_in(streams_of[3], 2), own, number, ROWS_DEV, N_BLK, 1, CAPP, 2))(owner_keys, owner_turns).reshape((TOKENS, 1))
    return {"rows": rows, "start_vec": start_vec, "leave": leave, "owner": owner}


def pack_rows(current, leaving, capacity):
    running = jnp.cumsum(leaving).astype(jnp.int32)
    slot_ids = jnp.arange(capacity, dtype=jnp.int32)
    source_idx = lax.optimization_barrier(jnp.sum((running[None, :] <= slot_ids[:, None]).astype(jnp.int32), axis=1))
    filled = slot_ids < running[-1]
    picked = jnp.take(current, jnp.minimum(source_idx, current.shape[0] - 1), axis=0)
    return jnp.where(filled[:, None], picked, jnp.zeros_like(picked))

def place_rows(current, leaving, arrived):
    arrival = jnp.cumsum(leaving).astype(jnp.int32) - 1
    fetched = jnp.take(arrived, jnp.clip(arrival, 0, arrived.shape[0] - 1), axis=0)
    return jnp.where(leaving[:, None] == 1, fetched, current)

def leaf_blocks(current, owners, targets, capacity):
    onehot = (owners[:, None] == jnp.arange(targets, dtype=jnp.int32)[None, :]).astype(jnp.int32)
    running = jnp.cumsum(onehot, axis=0)
    slot_ids = jnp.arange(capacity, dtype=jnp.int32)
    source_idx = lax.optimization_barrier(jnp.sum((running[None, :, :] <= slot_ids[:, None, None]).astype(jnp.int32), axis=1))
    filled = slot_ids[:, None] < running[-1][None, :]
    picked = jnp.take(current, jnp.minimum(source_idx.T, current.shape[0] - 1), axis=0)
    return jnp.where(filled.T[:, :, None], picked, jnp.zeros_like(picked))

def power_iterate(operate, row_sum, members, start_vec):
    direction = start_vec / jnp.sqrt(jnp.sum(start_vec * start_vec))
    for step_no in range(ITERS):
        along = jnp.dot(row_sum, direction, precision=lax.Precision.HIGHEST)
        image_vec = operate(direction) - row_sum * (along / members)
        direction = image_vec / jnp.sqrt(jnp.sum(image_vec * image_vec))
    return direction

def cube_stats(cube_rows):
    flattened = cube_rows.reshape(-1, D)
    gram_part = jnp.dot(flattened.T, flattened, preferred_element_type=jnp.float32)
    return (gram_part, lax.optimization_barrier(jnp.sum(flattened.astype(jnp.float32), axis=0)))

def reference(rows, start_vec, leave, owner):
    current = rows.reshape(N_CUBE, N_BLK, ROWS_DEV, D)
    cube_ids = jnp.arange(N_CUBE, dtype=jnp.int32)
    scores = []
    for tree_level in range(LEVELS):
        leaving = leave[tree_level].reshape(N_CUBE, N_BLK, ROWS_DEV)
        cube_grams, cube_sums = lax.map(cube_stats, current)
        cells_now = 1 << tree_level
        members = ROWS_DEV * N_BLK * (N_CUBE >> tree_level)
        directions = []
        offsets = []
        for cell_no in range(cells_now):
            selector = (cube_ids % cells_now == cell_no).astype(jnp.float32)
            gram_sum = lax.optimization_barrier(jnp.sum(cube_grams * selector[:, None, None], axis=0))
            row_sum = lax.optimization_barrier(jnp.sum(cube_sums * selector[:, None], axis=0))

            def operate(vector, matrix=gram_sum):
                return jnp.dot(matrix, vector, precision=lax.Precision.HIGHEST)
            direction = power_iterate(operate, row_sum, members, start_vec)
            directions.append(direction)
            offsets.append(jnp.dot(row_sum, direction, precision=lax.Precision.HIGHEST) / members)
        directions = jnp.stack(directions)[cube_ids % cells_now]
        offsets = jnp.stack(offsets)[cube_ids % cells_now]

        def project(pair_args):
            cube_rows, direction = pair_args
            return jnp.dot(cube_rows.astype(jnp.float32), direction, precision=lax.Precision.HIGHEST)
        projected = lax.map(project, (current, directions)) - offsets[:, None, None]
        scores.append(projected.reshape(-1))
        packer = jax.vmap(jax.vmap(partial(pack_rows, capacity=CAP)))
        packed = packer(current, leaving)
        arrived = packed[jnp.bitwise_xor(cube_ids, 1 << tree_level)]
        current = jax.vmap(jax.vmap(place_rows))(current, leaving, arrived)
    flattened = current.reshape(N_CUBE * N_BLK, ROWS_DEV, D)
    owners = owner.reshape(N_CUBE * N_BLK, ROWS_DEV)

    def route(pair_args):
        return leaf_blocks(pair_args[0], pair_args[1], N_BLK, CAPP)
    blocks = lax.map(route, (flattened, owners))
    blocks = blocks.reshape(N_CUBE, N_BLK, N_BLK, CAPP, D).transpose(0, 2, 1, 3, 4)
    return (jnp.stack(scores).astype(jnp.float32), blocks.reshape(-1, D))
```

```python
import jax
import jax.numpy as jnp
from jax import lax
from jax.experimental import pallas as pl
from jax.experimental.pallas import tpu as pltpu
from jax.sharding import PartitionSpec as P

D = 1024
ROWS = 1536
CAP = 768
CAPP = 192
N_BLK = 16
N_CUBE = 8
ITERS = 8
HALF = 512
LANES = 128
BLOCKS = [(i, j) for i in range(8) for j in range(i, 8)]
CHUNK = 9 * LANES
PIECE = CHUNK // 4
F32 = jnp.float32
BF16 = jnp.bfloat16
PARAMS = pltpu.CompilerParams(vmem_limit_bytes=56 * 2**20)
VMEM = pl.BlockSpec(memory_space=pltpu.VMEM)
SMEM = pl.BlockSpec(memory_space=pltpu.SMEM)
ANY = pl.BlockSpec(memory_space=pl.ANY)


def iota(shape, dim):
    return lax.broadcasted_iota(jnp.int32, shape, dim)


def shape_of(shape, dtype):
    return jax.ShapeDtypeStruct(shape, dtype)


def running_count(flags):
    upper = jnp.where(iota((LANES, LANES), 0) <= iota((LANES, LANES), 1), 1.0, 0.0).astype(BF16)
    parts = []
    before = jnp.zeros((flags.shape[0], 1), F32)
    for b in range(ROWS // LANES):
        part = flags[:, b * LANES : (b + 1) * LANES].astype(BF16)
        part = jnp.dot(part, upper, preferred_element_type=F32) + before
        before = part[:, LANES - 1 : LANES]
        parts.append(part)
    return jnp.concatenate(parts, axis=1)


def slot_row(leave_ref, level):
    flags = jnp.broadcast_to(leave_ref[level : level + 1, :].astype(F32), (8, ROWS))
    return jnp.where(flags > 0.5, running_count(flags) - 1.0, -1.0)


def store_column(row, col_ref):
    for b in range(ROWS // LANES):
        part = jnp.broadcast_to(row[0:1, b * LANES : (b + 1) * LANES], (LANES, LANES))
        col_ref[b * LANES : (b + 1) * LANES, :] = part.T


def picker(row, first, count):
    slots = (iota((count, ROWS), 0) + first).astype(F32)
    return jnp.where(slots == row[0:1, :], 1.0, 0.0).astype(BF16)


def spreader(col, slots):
    parts = []
    for t in range(slots // LANES):
        lanes = (iota(col.shape, 1) + t * LANES).astype(F32)
        parts.append(jnp.where(col == lanes, 1.0, 0.0).astype(BF16))
    return jnp.concatenate(parts, axis=1)


def pack_first_kernel(leave_ref, rows_ref, out_ref):
    row = slot_row(leave_ref, 0)
    for t in range(CAP // 256):
        hot = picker(row, t * 256, 256)
        out_ref[t * 256 : (t + 1) * 256, :] = jnp.dot(hot, rows_ref[...], preferred_element_type=F32).astype(BF16)


def pack_first(leave, rows, half):
    return pl.pallas_call(
        pack_first_kernel,
        grid=(1,),
        in_specs=[pl.BlockSpec((2, ROWS), lambda i: (0, 0)), pl.BlockSpec((ROWS, HALF), lambda i: (0, half))],
        out_specs=pl.BlockSpec((CAP, HALF), lambda i: (0, 0)),
        out_shape=shape_of((CAP, HALF), BF16),
        compiler_params=PARAMS,
        name="pack_first",
    )(leave, rows)


def slots_kernel(leave_ref, owner_ref, row_ref, col_ref):
    for level in range(2):
        row = slot_row(leave_ref, level)
        row_ref[level * 8 : (level + 1) * 8, :] = row
        store_column(row, col_ref.at[level])
    owner = jnp.broadcast_to(owner_ref[...], (N_BLK, ROWS))
    named = jnp.where(owner == iota((N_BLK, ROWS), 0), 1.0, 0.0)
    place = named * (running_count(named) - 1.0 + (iota((N_BLK, ROWS), 0) * CAPP).astype(F32))
    row_ref[16:24, :] = jnp.broadcast_to(jnp.sum(place, axis=0, keepdims=True), (8, ROWS))


def slots(leave, owner):
    return pl.pallas_call(
        slots_kernel,
        in_specs=[VMEM, VMEM],
        out_specs=[VMEM, VMEM],
        out_shape=[shape_of((24, ROWS), F32), shape_of((2, ROWS, LANES), F32)],
        compiler_params=PARAMS,
        name="slots",
    )(leave, owner)


def placed(col, arrived, stay):
    moved = jnp.dot(spreader(col, CAP), arrived, preferred_element_type=F32).astype(BF16)
    leaves = jnp.concatenate([col] * (HALF // LANES), axis=1) >= 0.0
    return jnp.where(leaves, moved.astype(F32), stay.astype(F32)).astype(BF16)


def swap_kernel(row_ref, col_ref, rows_ref, arrived_ref, next_ref, packed_ref):
    arrived = arrived_ref[...]
    for t in range(ROWS // 256):
        here = slice(t * 256, (t + 1) * 256)
        next_ref[here, :] = placed(col_ref[0, here, :], arrived, rows_ref[here, :])
    row = row_ref[8:16, :]
    for t in range(CAP // 256):
        hot = picker(row, t * 256, 256)
        packed_ref[t * 256 : (t + 1) * 256, :] = jnp.dot(hot, next_ref[...], preferred_element_type=F32).astype(BF16)


def swap(row, col, rows, arrived, half):
    whole = lambda shape: pl.BlockSpec(shape, lambda i: (0,) * len(shape))
    return pl.pallas_call(
        swap_kernel,
        grid=(1,),
        in_specs=[
            whole((24, ROWS)),
            whole((1, ROWS, LANES)),
            pl.BlockSpec((ROWS, HALF), lambda i: (0, half)),
            whole((CAP, HALF)),
        ],
        out_specs=[whole((ROWS, HALF)), whole((CAP, HALF))],
        out_shape=[shape_of((ROWS, HALF), BF16), shape_of((CAP, HALF), BF16)],
        compiler_params=PARAMS,
        name="swap",
    )(row, col, rows, arrived)


def leaf_kernel(row_ref, col_ref, rows_ref, arrived_ref, out_ref, last_ref):
    arrived = arrived_ref[...]
    for t in range(ROWS // 256):
        here = slice(t * 256, (t + 1) * 256)
        last_ref[here, :] = placed(col_ref[0, here, :], arrived, rows_ref[here, :])
    row = row_ref[16:24, :]
    for t in range(N_BLK * CAPP // 256):
        hot = picker(row, t * 256, 256)
        out_ref[t * 256 : (t + 1) * 256, :] = jnp.dot(hot, last_ref[...], preferred_element_type=F32).astype(BF16)


def leaf_pack(row, col, rows, arrived):
    whole = lambda shape: pl.BlockSpec(shape, lambda i: (0,) * len(shape))
    return pl.pallas_call(
        leaf_kernel,
        grid=(1,),
        in_specs=[
            whole((24, ROWS)),
            pl.BlockSpec((1, ROWS, LANES), lambda i: (1, 0, 0)),
            whole((ROWS, HALF)),
            whole((CAP, HALF)),
        ],
        out_specs=whole((N_BLK * CAPP, HALF)),
        out_shape=shape_of((N_BLK * CAPP, HALF), BF16),
        scratch_shapes=[pltpu.VMEM((ROWS, HALF), BF16)],
        compiler_params=PARAMS,
        name="leaf_pack",
    )(row, col, rows, arrived)


def gram_kernel(flip_ref, leave_ref, rows_ref, keep_ref, send_ref, turned_ref, masked_ref):
    turned_ref[...] = rows_ref[...].T
    flag = jnp.bitwise_xor(jnp.broadcast_to(leave_ref[0:1, :], (8, ROWS)), flip_ref[0]).astype(F32)
    lane = iota((8, LANES), 1)
    sub = iota((8, LANES), 0)
    for out_ref, weight in ((keep_ref, flag), (send_ref, 1.0 - flag)):
        masked_ref[...] = turned_ref[...] * weight[0:1, :].astype(BF16)
        sums = jnp.dot(weight.astype(BF16), rows_ref[...], preferred_element_type=F32)
        for r in range(4):
            strip = jnp.dot(
                masked_ref[r * 256 : (r + 1) * 256, :], rows_ref[:, r * 256 :], preferred_element_type=F32
            )
            for i in (2 * r, 2 * r + 1):
                for j in range(i, 8):
                    at = BLOCKS.index((i, j))
                    top = (at % 9) * LANES
                    out_ref[at // 9, top : top + LANES, :] = strip[
                        (i - 2 * r) * LANES : (i - 2 * r + 1) * LANES, (j - 2 * r) * LANES : (j - 2 * r + 1) * LANES
                    ]
        for i in range(8):
            at = BLOCKS.index((i, i))
            top = (at % 9) * LANES + 120
            own = sums[:, i * LANES : (i + 1) * LANES]
            held = jnp.where((sub == 7) & (lane < 64), own, out_ref[at // 9, top : top + 8, :])
            out_ref[at // 9, top : top + 8, :] = jnp.where((sub == 6) & (lane < 64), pltpu.roll(own, 64, 1), held)


def gram(flip, leave, rows):
    return pl.pallas_call(
        gram_kernel,
        in_specs=[SMEM, VMEM, VMEM],
        out_specs=[VMEM, VMEM],
        out_shape=[shape_of((4, CHUNK, LANES), F32)] * 2,
        scratch_shapes=[pltpu.VMEM((D, ROWS), BF16)] * 2,
        compiler_params=PARAMS,
        name="gram",
    )(flip, leave, rows)


def power_kernel(place_ref, members_ref, start_ref, a_ref, b_ref, c_ref, d_ref, out_ref, packed_ref, mat_ref):
    y, z = place_ref[0], place_ref[1]
    for k, part_ref in enumerate((a_ref, b_ref, c_ref, d_ref)):
        for m in range(4):
            at = (lax.rem(y + m, 4) * 4 + lax.rem(z + k, 4)) * PIECE
            packed_ref[pl.ds(pl.multiple_of(at, 8), PIECE), :] = part_ref[m]
    members = members_ref[0]
    lane = iota((8, LANES), 1)
    wide_lane, wide_sub = iota((LANES, LANES), 1), iota((LANES, LANES), 0)
    sums_row, sums_col = [], []
    for i in range(8):
        top = BLOCKS.index((i, i)) * LANES
        tail = packed_ref[top + 120 : top + 128, :]
        row = jnp.where(lane[0:1] < 64, tail[7:8, :], pltpu.roll(tail, 64, 1)[6:7, :])
        sums_row.append(row)
        sums_col.append(jnp.broadcast_to(row, (LANES, LANES)).T)
    for i in range(8):
        for j in range(i, 8):
            top = BLOCKS.index((i, j)) * LANES
            block = packed_ref[top : top + LANES, :]
            other = block.T
            if i == j:
                block = jnp.where((wide_sub >= 126) & (wide_lane < 64), other, block)
            hi, hj = slice(i * LANES, (i + 1) * LANES), slice(j * LANES, (j + 1) * LANES)
            mat_ref[hi, hj] = block - sums_col[i] * (sums_row[j] / members)
            if i != j:
                mat_ref[hj, hi] = other - sums_col[j] * (sums_row[i] / members)
    start = start_ref[...]
    vec = start / jnp.sqrt(jnp.sum(start * start, axis=1, keepdims=True))
    for _ in range(ITERS // 2):
        cols = []
        square = jnp.zeros((8, 1), F32)
        for i in range(8):
            total = jnp.zeros((LANES, LANES), F32)
            for j in range(8):
                total = total + mat_ref[i * LANES : (i + 1) * LANES, j * LANES : (j + 1) * LANES] * vec[
                    :, j * LANES : (j + 1) * LANES
                ]
            col = jnp.sum(total, axis=1, keepdims=True)
            cols.append(col)
        norm = sum(jnp.sum(col * col, axis=0, keepdims=True) for col in cols)
        norm = jnp.sqrt(norm)
        total = jnp.zeros((8, D), F32)
        for i in range(8):
            col = cols[i] / norm
            for s in range(LANES // 8):
                at = i * LANES + s * 8
                total = total + mat_ref[at : at + 8, :] * col[s * 8 : (s + 1) * 8, :]
        vec = jnp.sum(total, axis=0, keepdims=True)
        vec = vec / jnp.sqrt(jnp.sum(vec * vec, axis=1, keepdims=True))
    sums = jnp.concatenate(sums_row, axis=1)
    offset = jnp.sum(sums * vec, axis=1, keepdims=True) / members
    out_ref[0:8, :] = jnp.where(iota((8, D), 0) == 0, vec, offset)


def power(place, members, start, parts):
    return pl.pallas_call(
        power_kernel,
        in_specs=[SMEM, SMEM, VMEM] + [VMEM] * 4,
        out_specs=VMEM,
        out_shape=shape_of((8, D), F32),
        scratch_shapes=[pltpu.VMEM((len(BLOCKS) * LANES, LANES), F32), pltpu.VMEM((D, D), F32)],
        compiler_params=PARAMS,
        name="power",
    )(place, members, start, *parts)


def project(vec, blocks):
    sub = None
    total = None
    at = 0
    for block in blocks:
        here = vec[:, at : at + block.shape[1]]
        at += block.shape[1]
        high = here.astype(BF16)
        rest = here - high.astype(F32)
        mid = rest.astype(BF16)
        low = (rest - mid.astype(F32)).astype(BF16)
        sub = iota((8, here.shape[1]), 0)
        terms = jnp.where(
            sub == 0,
            high.astype(F32),
            jnp.where(sub == 1, mid.astype(F32), jnp.where(sub == 2, low.astype(F32), 0.0)),
        ).astype(BF16)
        part = lax.dot_general(terms, block, (((1,), (1,)), ((), ())), preferred_element_type=F32)
        total = part if total is None else total + part
    return total[0:1, :] + total[1:2, :] + total[2:3, :]


def scores_kernel(core_ref, mine_ref, other_ref, rows_ref, left_ref, right_ref, out_ref):
    first = core_ref[0] == 0
    top = jnp.where(first, mine_ref[...], other_ref[...])
    low = jnp.where(first, other_ref[...], mine_ref[...])
    out_ref[0:1, :] = project(top[0:1, :], [rows_ref[...]]) - top[1:2, 0:1]
    out_ref[1:2, :] = project(low[0:1, :], [left_ref[...], right_ref[...]]) - low[1:2, 0:1]


def all_scores(core, mine, other, rows, left, right):
    return pl.pallas_call(
        scores_kernel,
        in_specs=[SMEM] + [VMEM] * 5,
        out_specs=VMEM,
        out_shape=shape_of((2, ROWS), F32),
        compiler_params=PARAMS,
        name="scores",
    )(core, mine, other, rows, left, right)


def join_first_kernel(part_ref, out_ref):
    out_ref[...] = part_ref[...]


def join_second_kernel(part_ref, held_ref, out_ref):
    out_ref[...] = part_ref[...]


def join(left, right):
    count = left.shape[0]
    block = pl.BlockSpec((512, HALF), lambda i: (i, 0))
    held = pl.pallas_call(
        join_first_kernel,
        grid=(count // 512,),
        in_specs=[block],
        out_specs=pl.BlockSpec((512, HALF), lambda i: (i, 0)),
        out_shape=shape_of((count, D), BF16),
        compiler_params=PARAMS,
        name="join_first",
    )(left)
    return pl.pallas_call(
        join_second_kernel,
        grid=(count // 512,),
        in_specs=[block, ANY],
        out_specs=pl.BlockSpec((512, HALF), lambda i: (i, 1)),
        out_shape=shape_of((count, D), BF16),
        input_output_aliases={1: 0},
        compiler_params=PARAMS,
        name="join_second",
    )(right, held)


def along_y(value, k):
    return lax.ppermute(value, "blk", [(i, (i // 4 + k) % 4 * 4 + i % 4) for i in range(N_BLK)])


def along_z(value, k):
    return lax.ppermute(value, "cube", [(i, (i // 2 + k) % 4 * 2 + i % 2) for i in range(N_CUBE)])


def across(value, axis, bit):
    return lax.ppermute(value, axis, [(i, i ^ bit) for i in range(lax.axis_size(axis))])


def after(value, earlier):
    return lax.optimization_barrier((value, earlier))[0]


def per_device(rows, start_vec, leave, owner):
    cube, blk = lax.axis_index("cube"), lax.axis_index("blk")
    z, x_lo = cube // 2, cube % 2
    y, core = blk // 4, blk % 2

    packed_l = pack_first(leave, rows, 0)
    arrived_l = across(packed_l, "cube", 1)
    packed_r = pack_first(leave, rows, 1)

    flip = jnp.bitwise_xor(x_lo, core).astype(jnp.int32).reshape(1)
    keep, send = gram(flip, leave, rows)
    got = across(send, "blk", 1)
    row, col = slots(leave, owner.reshape(1, ROWS))

    def part(k):
        at = (y + k) % 4
        return lax.dynamic_index_in_dim(keep, at, 0, False) + lax.dynamic_index_in_dim(got, at, 0, False)

    parts = [part(k) for k in range(4)]
    own = parts[0]
    for k in (1, 2, 3):
        own = own + along_y(parts[k], k)
    quarters = own.reshape(4, PIECE, LANES)
    own = lax.dynamic_index_in_dim(quarters, z, 0, False)
    for k in (1, 2, 3):
        own = own + along_z(lax.dynamic_index_in_dim(quarters, (z + k) % 4, 0, False), k)
    own = own + across(own, "cube", 1)
    own = own + across(own, "blk", 2)
    other = across(own, "blk", 1)
    piece = jnp.where(core == 0, own + other, jnp.where(x_lo == 0, own, other))
    stack = jnp.stack([piece] + [along_y(piece, -k) for k in (1, 2, 3)])
    gathered = [stack] + [along_z(stack, -k) for k in (1, 2, 3)]

    packed_r = after(packed_r, arrived_l)
    arrived_r = across(packed_r, "cube", 1)
    next_l, packed_l = swap(row, col, rows, arrived_l, 0)
    arrived2_l = across(packed_l, "cube", 2)
    next_r, packed_r = swap(row, col, rows, arrived_r, 1)
    packed_r = after(packed_r, arrived2_l)
    arrived2_r = across(packed_r, "cube", 2)
    leaf_l = leaf_pack(row, col, next_l, arrived2_l)
    out_l = lax.all_to_all(leaf_l, "blk", split_axis=0, concat_axis=0, tiled=True)
    leaf_r = leaf_pack(row, col, next_r, arrived2_r)
    out_r = lax.all_to_all(leaf_r, "blk", split_axis=0, concat_axis=0, tiled=True)

    place = jnp.stack([y, z]).astype(jnp.int32)
    members = jnp.where(core == 0, ROWS * N_BLK * N_CUBE, ROWS * N_BLK * N_CUBE // 2).astype(F32).reshape(1)
    mine = power(place, members, start_vec.reshape(1, D), gathered)
    theirs = across(mine, "blk", 1)
    scores = all_scores(core.astype(jnp.int32).reshape(1), mine, theirs, rows, next_l, next_r)
    return scores, join(out_l, out_r)


def solution(mesh):
    placed_at = (P(("cube", "blk"), None), P(), P(None, ("cube", "blk")), P(("cube", "blk"), None))
    return jax.shard_map(
        per_device,
        mesh=mesh,
        in_specs=placed_at,
        out_specs=(P(None, ("cube", "blk")), P(("cube", "blk"), None)),
        check_vma=False,
    )
```

```python
import jax
import jax.numpy as jnp
from jax import lax
from jax.experimental import pallas as pl
from jax.experimental.pallas import tpu as pltpu
from jax.sharding import PartitionSpec as P

D = 1024
ROWS = 1536
CAP = 768
CAPP = 192
N_BLK = 16
N_CUBE = 8
ITERS = 8
HALF = 512
LANES = 128
BLOCKS = [(i, j) for i in range(8) for j in range(i, 8)]
CHUNK = 9 * LANES
PIECE = CHUNK // 4
F32 = jnp.float32
BF16 = jnp.bfloat16
PARAMS = pltpu.CompilerParams(vmem_limit_bytes=56 * 2**20)


def cost(microseconds):
    return pl.CostEstimate(
        flops=int(microseconds * 1.15e9), bytes_accessed=int(microseconds * 3.69e6), transcendentals=0
    )


VMEM = pl.BlockSpec(memory_space=pltpu.VMEM)
SMEM = pl.BlockSpec(memory_space=pltpu.SMEM)
ANY = pl.BlockSpec(memory_space=pl.ANY)


def iota(shape, dim):
    return lax.broadcasted_iota(jnp.int32, shape, dim)


def shape_of(shape, dtype):
    return jax.ShapeDtypeStruct(shape, dtype)


def running_count(flags):
    upper = jnp.where(iota((LANES, LANES), 0) <= iota((LANES, LANES), 1), 1.0, 0.0).astype(BF16)
    parts = []
    before = jnp.zeros((flags.shape[0], 1), F32)
    for b in range(ROWS // LANES):
        part = flags[:, b * LANES : (b + 1) * LANES].astype(BF16)
        part = jnp.dot(part, upper, preferred_element_type=F32) + before
        before = part[:, LANES - 1 : LANES]
        parts.append(part)
    return jnp.concatenate(parts, axis=1)


def slot_row(leave_ref, level):
    flags = jnp.broadcast_to(leave_ref[level : level + 1, :].astype(F32), (8, ROWS))
    return jnp.where(flags > 0.5, running_count(flags) - 1.0, -1.0)


def store_column(row, col_ref):
    for b in range(ROWS // LANES):
        part = jnp.broadcast_to(row[0:1, b * LANES : (b + 1) * LANES], (LANES, LANES))
        col_ref[b * LANES : (b + 1) * LANES, :] = part.T


def picker(row, first, count):
    slots = (iota((count, ROWS), 0) + first).astype(F32)
    return jnp.where(slots == row[0:1, :], 1.0, 0.0).astype(BF16)


def spreader(col, slots):
    parts = []
    for t in range(slots // LANES):
        lanes = (iota(col.shape, 1) + t * LANES).astype(F32)
        parts.append(jnp.where(col == lanes, 1.0, 0.0).astype(BF16))
    return jnp.concatenate(parts, axis=1)


def pack_first_kernel(leave_ref, rows_ref, out_ref):
    row = slot_row(leave_ref, 0)
    for t in range(CAP // 256):
        hot = picker(row, t * 256, 256)
        out_ref[t * 256 : (t + 1) * 256, :] = jnp.dot(hot, rows_ref[...], preferred_element_type=F32).astype(BF16)


def pack_first(leave, rows, half):
    return pl.pallas_call(
        pack_first_kernel,
        grid=(1,),
        in_specs=[pl.BlockSpec((2, ROWS), lambda i: (0, 0)), pl.BlockSpec((ROWS, HALF), lambda i: (0, half))],
        out_specs=pl.BlockSpec((CAP, HALF), lambda i: (0, 0)),
        out_shape=shape_of((CAP, HALF), BF16),
        compiler_params=PARAMS,
        cost_estimate=cost(4.3),
        name="pack_first",
    )(leave, rows)


def slots_kernel(leave_ref, owner_ref, row_ref, col_ref):
    for level in range(2):
        row = slot_row(leave_ref, level)
        row_ref[level * 8 : (level + 1) * 8, :] = row
        store_column(row, col_ref.at[level])
    owner = jnp.broadcast_to(owner_ref[...], (N_BLK, ROWS))
    named = jnp.where(owner == iota((N_BLK, ROWS), 0), 1.0, 0.0)
    place = named * (running_count(named) - 1.0 + (iota((N_BLK, ROWS), 0) * CAPP).astype(F32))
    row_ref[16:24, :] = jnp.broadcast_to(jnp.sum(place, axis=0, keepdims=True), (8, ROWS))


def slots(leave, owner):
    return pl.pallas_call(
        slots_kernel,
        in_specs=[VMEM, VMEM],
        out_specs=[VMEM, VMEM],
        out_shape=[shape_of((24, ROWS), F32), shape_of((2, ROWS, LANES), F32)],
        compiler_params=PARAMS,
        cost_estimate=cost(3.2),
        name="slots",
    )(leave, owner)


def placed(col, arrived, stay):
    moved = jnp.dot(spreader(col, CAP), arrived, preferred_element_type=F32).astype(BF16)
    leaves = jnp.concatenate([col] * (HALF // LANES), axis=1) >= 0.0
    return jnp.where(leaves, moved.astype(F32), stay.astype(F32)).astype(BF16)


def swap_kernel(row_ref, col_ref, rows_ref, arrived_ref, next_ref, packed_ref):
    arrived = arrived_ref[...]
    for t in range(ROWS // 256):
        here = slice(t * 256, (t + 1) * 256)
        next_ref[here, :] = placed(col_ref[0, here, :], arrived, rows_ref[here, :])
    row = row_ref[8:16, :]
    for t in range(CAP // 256):
        hot = picker(row, t * 256, 256)
        packed_ref[t * 256 : (t + 1) * 256, :] = jnp.dot(hot, next_ref[...], preferred_element_type=F32).astype(BF16)


def swap(row, col, rows, arrived, half):
    whole = lambda shape: pl.BlockSpec(shape, lambda i: (0,) * len(shape))
    return pl.pallas_call(
        swap_kernel,
        grid=(1,),
        in_specs=[
            whole((24, ROWS)),
            whole((1, ROWS, LANES)),
            pl.BlockSpec((ROWS, HALF), lambda i: (0, half)),
            whole((CAP, HALF)),
        ],
        out_specs=[whole((ROWS, HALF)), whole((CAP, HALF))],
        out_shape=[shape_of((ROWS, HALF), BF16), shape_of((CAP, HALF), BF16)],
        compiler_params=PARAMS,
        cost_estimate=cost(20.0 if half == 0 else 5.3),
        name="swap",
    )(row, col, rows, arrived)


def leaf_kernel(row_ref, col_ref, rows_ref, arrived_ref, out_ref, last_ref):
    arrived = arrived_ref[...]
    for t in range(ROWS // 256):
        here = slice(t * 256, (t + 1) * 256)
        last_ref[here, :] = placed(col_ref[0, here, :], arrived, rows_ref[here, :])
    row = row_ref[16:24, :]
    for t in range(N_BLK * CAPP // 256):
        hot = picker(row, t * 256, 256)
        out_ref[t * 256 : (t + 1) * 256, :] = jnp.dot(hot, last_ref[...], preferred_element_type=F32).astype(BF16)


def leaf_pack(row, col, rows, arrived):
    whole = lambda shape: pl.BlockSpec(shape, lambda i: (0,) * len(shape))
    return pl.pallas_call(
        leaf_kernel,
        grid=(1,),
        in_specs=[
            whole((24, ROWS)),
            pl.BlockSpec((1, ROWS, LANES), lambda i: (1, 0, 0)),
            whole((ROWS, HALF)),
            whole((CAP, HALF)),
        ],
        out_specs=whole((N_BLK * CAPP, HALF)),
        out_shape=shape_of((N_BLK * CAPP, HALF), BF16),
        scratch_shapes=[pltpu.VMEM((ROWS, HALF), BF16)],
        compiler_params=PARAMS,
        cost_estimate=cost(9.8),
        name="leaf_pack",
    )(row, col, rows, arrived)


def gram_kernel(flip_ref, leave_ref, rows_ref, keep_ref, send_ref, turned_ref, masked_ref):
    turned_ref[...] = rows_ref[...].T
    flag = jnp.bitwise_xor(jnp.broadcast_to(leave_ref[0:1, :], (8, ROWS)), flip_ref[0]).astype(F32)
    lane = iota((8, LANES), 1)
    sub = iota((8, LANES), 0)
    for out_ref, weight in ((keep_ref, flag), (send_ref, 1.0 - flag)):
        masked_ref[...] = turned_ref[...] * weight[0:1, :].astype(BF16)
        sums = jnp.dot(weight.astype(BF16), rows_ref[...], preferred_element_type=F32)
        for r in range(4):
            strip = jnp.dot(
                masked_ref[r * 256 : (r + 1) * 256, :], rows_ref[:, r * 256 :], preferred_element_type=F32
            )
            for i in (2 * r, 2 * r + 1):
                for j in range(i, 8):
                    at = BLOCKS.index((i, j))
                    top = (at % 9) * LANES
                    out_ref[at // 9, top : top + LANES, :] = strip[
                        (i - 2 * r) * LANES : (i - 2 * r + 1) * LANES, (j - 2 * r) * LANES : (j - 2 * r + 1) * LANES
                    ]
        for i in range(8):
            at = BLOCKS.index((i, i))
            top = (at % 9) * LANES + 120
            own = sums[:, i * LANES : (i + 1) * LANES]
            held = jnp.where((sub == 7) & (lane < 64), own, out_ref[at // 9, top : top + 8, :])
            out_ref[at // 9, top : top + 8, :] = jnp.where((sub == 6) & (lane < 64), pltpu.roll(own, 64, 1), held)


def gram(flip, leave, rows):
    return pl.pallas_call(
        gram_kernel,
        in_specs=[SMEM, VMEM, VMEM],
        out_specs=[VMEM, VMEM],
        out_shape=[shape_of((4, CHUNK, LANES), F32)] * 2,
        scratch_shapes=[pltpu.VMEM((D, ROWS), BF16)] * 2,
        compiler_params=PARAMS,
        cost_estimate=cost(8.6),
        name="gram",
    )(flip, leave, rows)


def power_kernel(place_ref, members_ref, start_ref, a_ref, b_ref, c_ref, d_ref, out_ref, packed_ref, mat_ref):
    y, z = place_ref[0], place_ref[1]
    for k, part_ref in enumerate((a_ref, b_ref, c_ref, d_ref)):
        for m in range(4):
            at = (lax.rem(y + m, 4) * 4 + lax.rem(z + k, 4)) * PIECE
            packed_ref[pl.ds(pl.multiple_of(at, 8), PIECE), :] = part_ref[m]
    members = members_ref[0]
    lane = iota((8, LANES), 1)
    wide_lane, wide_sub = iota((LANES, LANES), 1), iota((LANES, LANES), 0)
    sums_row, sums_col = [], []
    for i in range(8):
        top = BLOCKS.index((i, i)) * LANES
        tail = packed_ref[top + 120 : top + 128, :]
        row = jnp.where(lane[0:1] < 64, tail[7:8, :], pltpu.roll(tail, 64, 1)[6:7, :])
        sums_row.append(row)
        sums_col.append(jnp.broadcast_to(row, (LANES, LANES)).T)
    for i in range(8):
        for j in range(i, 8):
            top = BLOCKS.index((i, j)) * LANES
            block = packed_ref[top : top + LANES, :]
            other = block.T
            if i == j:
                block = jnp.where((wide_sub >= 126) & (wide_lane < 64), other, block)
            hi, hj = slice(i * LANES, (i + 1) * LANES), slice(j * LANES, (j + 1) * LANES)
            mat_ref[hi, hj] = block - sums_col[i] * (sums_row[j] / members)
            if i != j:
                mat_ref[hj, hi] = other - sums_col[j] * (sums_row[i] / members)
    start = start_ref[...]
    vec = start / jnp.sqrt(jnp.sum(start * start, axis=1, keepdims=True))
    for _ in range(ITERS // 2):
        cols = []
        square = jnp.zeros((8, 1), F32)
        for i in range(8):
            total = jnp.zeros((LANES, LANES), F32)
            for j in range(8):
                total = total + mat_ref[i * LANES : (i + 1) * LANES, j * LANES : (j + 1) * LANES] * vec[
                    :, j * LANES : (j + 1) * LANES
                ]
            col = jnp.sum(total, axis=1, keepdims=True)
            cols.append(col)
        norm = sum(jnp.sum(col * col, axis=0, keepdims=True) for col in cols)
        norm = jnp.sqrt(norm)
        total = jnp.zeros((8, D), F32)
        for i in range(8):
            col = cols[i] / norm
            for s in range(LANES // 8):
                at = i * LANES + s * 8
                total = total + mat_ref[at : at + 8, :] * col[s * 8 : (s + 1) * 8, :]
        vec = jnp.sum(total, axis=0, keepdims=True)
        vec = vec / jnp.sqrt(jnp.sum(vec * vec, axis=1, keepdims=True))
    sums = jnp.concatenate(sums_row, axis=1)
    offset = jnp.sum(sums * vec, axis=1, keepdims=True) / members
    out_ref[0:8, :] = jnp.where(iota((8, D), 0) == 0, vec, offset)


def power(place, members, start, parts):
    return pl.pallas_call(
        power_kernel,
        in_specs=[SMEM, SMEM, VMEM] + [VMEM] * 4,
        out_specs=VMEM,
        out_shape=shape_of((8, D), F32),
        scratch_shapes=[pltpu.VMEM((len(BLOCKS) * LANES, LANES), F32), pltpu.VMEM((D, D), F32)],
        compiler_params=PARAMS,
        cost_estimate=cost(6.6),
        name="power",
    )(place, members, start, *parts)


def project(vec, blocks):
    sub = None
    total = None
    at = 0
    for block in blocks:
        here = vec[:, at : at + block.shape[1]]
        at += block.shape[1]
        high = here.astype(BF16)
        rest = here - high.astype(F32)
        mid = rest.astype(BF16)
        low = (rest - mid.astype(F32)).astype(BF16)
        sub = iota((8, here.shape[1]), 0)
        terms = jnp.where(
            sub == 0,
            high.astype(F32),
            jnp.where(sub == 1, mid.astype(F32), jnp.where(sub == 2, low.astype(F32), 0.0)),
        ).astype(BF16)
        part = lax.dot_general(terms, block, (((1,), (1,)), ((), ())), preferred_element_type=F32)
        total = part if total is None else total + part
    return total[0:1, :] + total[1:2, :] + total[2:3, :]


def scores_kernel(core_ref, mine_ref, other_ref, rows_ref, left_ref, right_ref, out_ref):
    first = core_ref[0] == 0
    top = jnp.where(first, mine_ref[...], other_ref[...])
    low = jnp.where(first, other_ref[...], mine_ref[...])
    out_ref[0:1, :] = project(top[0:1, :], [rows_ref[...]]) - top[1:2, 0:1]
    out_ref[1:2, :] = project(low[0:1, :], [left_ref[...], right_ref[...]]) - low[1:2, 0:1]


def all_scores(core, mine, other, rows, left, right):
    return pl.pallas_call(
        scores_kernel,
        in_specs=[SMEM] + [VMEM] * 5,
        out_specs=VMEM,
        out_shape=shape_of((2, ROWS), F32),
        compiler_params=PARAMS,
        cost_estimate=cost(5.2),
        name="scores",
    )(core, mine, other, rows, left, right)


def join_first_kernel(part_ref, out_ref):
    out_ref[...] = part_ref[...]


def join_second_kernel(part_ref, held_ref, out_ref):
    out_ref[...] = part_ref[...]


JOIN = 512


def join_first(left):
    return pl.pallas_call(
        join_first_kernel,
        grid=(N_BLK * CAPP // JOIN,),
        in_specs=[pl.BlockSpec((JOIN, HALF), lambda i: (i, 0))],
        out_specs=pl.BlockSpec((JOIN, HALF), lambda i: (i, 0)),
        out_shape=shape_of((N_BLK * CAPP, D), BF16),
        compiler_params=PARAMS,
        cost_estimate=cost(5.2),
        name="join_first",
    )(left)


def join_second(right, held):
    return pl.pallas_call(
        join_second_kernel,
        grid=(N_BLK * CAPP // JOIN,),
        in_specs=[pl.BlockSpec((JOIN, HALF), lambda i: (i, 0)), ANY],
        out_specs=pl.BlockSpec((JOIN, HALF), lambda i: (i, 1)),
        out_shape=shape_of((N_BLK * CAPP, D), BF16),
        input_output_aliases={1: 0},
        compiler_params=PARAMS,
        cost_estimate=cost(5.2),
        name="join_second",
    )(right, held)


def along_y(value, k):
    return lax.ppermute(value, "blk", [(i, (i // 4 + k) % 4 * 4 + i % 4) for i in range(N_BLK)])


def along_z(value, k):
    return lax.ppermute(value, "cube", [(i, (i // 2 + k) % 4 * 2 + i % 2) for i in range(N_CUBE)])


def along_x(value, k):
    pairs = []
    for i in range(N_CUBE * N_BLK):
        cube, blk = i // N_BLK, i % N_BLK
        x = (blk // 2 % 2 * 2 + cube % 2 + k) % 4
        pairs.append((i, (cube // 2 * 2 + x % 2) * N_BLK + blk // 4 * 4 + x // 2 * 2 + blk % 2))
    return lax.ppermute(value, ("cube", "blk"), pairs)


def across(value, axis, bit):
    return lax.ppermute(value, axis, [(i, i ^ bit) for i in range(lax.axis_size(axis))])


def after(value, earlier):
    return lax.optimization_barrier((value, earlier))[0]


def per_device(rows, start_vec, leave, owner):
    cube, blk = lax.axis_index("cube"), lax.axis_index("blk")
    z, x_lo = cube // 2, cube % 2
    y, core = blk // 4, blk % 2

    packed_l = pack_first(leave, rows, 0)
    arrived_l = across(packed_l, "cube", 1)
    leave_b = after(leave, packed_l)
    packed_r = pack_first(leave_b, rows, 1)
    row, col = slots(leave_b, owner.reshape(1, ROWS))

    flip = jnp.bitwise_xor(x_lo, core).astype(jnp.int32).reshape(1)
    leave_c, packed_r, row = lax.optimization_barrier((leave, packed_r, row))
    keep, send = gram(flip, leave_c, rows)
    got = across(send, "blk", 1)

    packed_r, arrived_l, keep = lax.optimization_barrier((packed_r, arrived_l, keep))
    arrived_r = across(packed_r, "cube", 1)
    next_l, packed_l = swap(row, col, rows, arrived_l, 0)
    arrived2_l = across(packed_l, "cube", 2)

    got = after(got, packed_l)

    def part(k):
        at = (y + k) % 4
        return lax.dynamic_index_in_dim(keep, at, 0, False) + lax.dynamic_index_in_dim(got, at, 0, False)

    parts = lax.optimization_barrier([part(k) for k in range(4)])
    moved = [along_y(parts[k], k) for k in (1, 2, 3)]

    next_r, packed_r = swap(row, col, rows, after(arrived_r, parts), 1)
    arrived2_r = across(packed_r, "cube", 2)
    leaf_l = leaf_pack(row, col, next_l, after(arrived2_l, packed_r))

    moved, _, arrived2_r = lax.optimization_barrier((moved, leaf_l, arrived2_r))
    out_l = lax.all_to_all(leaf_l, "blk", split_axis=0, concat_axis=0, tiled=True)
    own = parts[0] + moved[0] + moved[1] + moved[2]
    quarters = own.reshape(4, PIECE, LANES)
    parts = lax.optimization_barrier(
        [lax.dynamic_index_in_dim(quarters, (z + k) % 4, 0, False) for k in range(4)]
    )
    moved = [along_z(parts[k], k) for k in (1, 2, 3)]

    leaf_r = leaf_pack(row, col, next_r, after(arrived2_r, parts))

    moved = after(moved, leaf_r)
    own = parts[0] + moved[0] + moved[1] + moved[2]
    other = across(own, "blk", 1)
    both = own + other
    mine = jnp.where(core == 0, both, jnp.where(x_lo == 0, own, other))
    theirs = jnp.where(core == 0, both, jnp.where(x_lo == 0, other, own))
    mine, theirs, out_l = lax.optimization_barrier((mine, theirs, out_l))
    piece = mine + along_x(mine, 2) + along_x(theirs, 1) + along_x(theirs, 3)
    near = [along_y(piece, -k) for k in (1, 2, 3)]
    near, leaf_r, out_l = lax.optimization_barrier((near, leaf_r, out_l))
    out_r = lax.all_to_all(leaf_r, "blk", split_axis=0, concat_axis=0, tiled=True)
    stack = jnp.stack([piece] + near)
    gathered = [stack] + [along_z(stack, -k) for k in (1, 2, 3)]
    held = join_first(after(out_l, stack))
    held, gathered = lax.optimization_barrier((held, gathered))

    place = jnp.stack([y, z]).astype(jnp.int32)
    members = jnp.where(core == 0, ROWS * N_BLK * N_CUBE, ROWS * N_BLK * N_CUBE // 2).astype(F32).reshape(1)
    mine = power(place, members, start_vec.reshape(1, D), gathered)
    theirs = across(mine, "blk", 1)
    scores = all_scores(core.astype(jnp.int32).reshape(1), mine, theirs, rows, next_l, next_r)
    return scores, join_second(out_r, held)


def solution(mesh):
    placed_at = (P(("cube", "blk"), None), P(), P(None, ("cube", "blk")), P(("cube", "blk"), None))
    return jax.shard_map(
        per_device,
        mesh=mesh,
        in_specs=placed_at,
        out_specs=(P(None, ("cube", "blk")), P(("cube", "blk"), None)),
        check_vma=False,
    )
```

```python
import jax
import jax.numpy as jnp
from jax import lax
from jax.experimental import pallas as pl
from jax.experimental.pallas import tpu as pltpu
from jax.sharding import PartitionSpec as P

D = 1024
ROWS = 1536
CAP = 768
CAPP = 192
N_BLK = 16
N_CUBE = 8
ITERS = 8
HALF = 512
LANES = 128
BLOCKS = [(i, j) for i in range(8) for j in range(i, 8)]
CHUNK = 9 * LANES
PIECE = CHUNK // 4
F32 = jnp.float32
BF16 = jnp.bfloat16
PARAMS = pltpu.CompilerParams(vmem_limit_bytes=56 * 2**20)


def cost(microseconds):
    return pl.CostEstimate(
        flops=int(microseconds * 1.15e9), bytes_accessed=int(microseconds * 3.69e6), transcendentals=0
    )


VMEM = pl.BlockSpec(memory_space=pltpu.VMEM)
SMEM = pl.BlockSpec(memory_space=pltpu.SMEM)
ANY = pl.BlockSpec(memory_space=pl.ANY)


def iota(shape, dim):
    return lax.broadcasted_iota(jnp.int32, shape, dim)


def shape_of(shape, dtype):
    return jax.ShapeDtypeStruct(shape, dtype)


def running_count(flags):
    upper = jnp.where(iota((LANES, LANES), 0) <= iota((LANES, LANES), 1), 1.0, 0.0).astype(BF16)
    parts = []
    before = jnp.zeros((flags.shape[0], 1), F32)
    for b in range(ROWS // LANES):
        part = flags[:, b * LANES : (b + 1) * LANES].astype(BF16)
        part = jnp.dot(part, upper, preferred_element_type=F32) + before
        before = part[:, LANES - 1 : LANES]
        parts.append(part)
    return jnp.concatenate(parts, axis=1)


def slot_row(leave_ref, level):
    flags = jnp.broadcast_to(leave_ref[level : level + 1, :].astype(F32), (8, ROWS))
    return jnp.where(flags > 0.5, running_count(flags) - 1.0, -1.0)


def store_column(row, col_ref):
    for b in range(ROWS // LANES):
        part = jnp.broadcast_to(row[0:1, b * LANES : (b + 1) * LANES], (LANES, LANES))
        col_ref[b * LANES : (b + 1) * LANES, :] = part.T


def picker(row, first, count):
    slots = (iota((count, ROWS), 0) + first).astype(F32)
    return jnp.where(slots == row[0:1, :], 1.0, 0.0).astype(BF16)


def spreader(col, slots):
    parts = []
    for t in range(slots // LANES):
        lanes = (iota(col.shape, 1) + t * LANES).astype(F32)
        parts.append(jnp.where(col == lanes, 1.0, 0.0).astype(BF16))
    return jnp.concatenate(parts, axis=1)


def pack_first_kernel(leave_ref, rows_ref, out_ref):
    row = slot_row(leave_ref, 0)
    for t in range(CAP // 256):
        hot = picker(row, t * 256, 256)
        out_ref[t * 256 : (t + 1) * 256, :] = jnp.dot(hot, rows_ref[...], preferred_element_type=F32).astype(BF16)


def pack_first(leave, rows, half):
    return pl.pallas_call(
        pack_first_kernel,
        grid=(1,),
        in_specs=[pl.BlockSpec((2, ROWS), lambda i: (0, 0)), pl.BlockSpec((ROWS, HALF), lambda i: (0, half))],
        out_specs=pl.BlockSpec((CAP, HALF), lambda i: (0, 0)),
        out_shape=shape_of((CAP, HALF), BF16),
        compiler_params=PARAMS,
        cost_estimate=cost(4.3),
        name="pack_first",
    )(leave, rows)


def slots_kernel(leave_ref, owner_ref, row_ref, col_ref):
    for level in range(2):
        row = slot_row(leave_ref, level)
        row_ref[level * 8 : (level + 1) * 8, :] = row
        store_column(row, col_ref.at[level])
    owner = jnp.broadcast_to(owner_ref[...], (N_BLK, ROWS))
    named = jnp.where(owner == iota((N_BLK, ROWS), 0), 1.0, 0.0)
    place = named * (running_count(named) - 1.0 + (iota((N_BLK, ROWS), 0) * CAPP).astype(F32))
    row_ref[16:24, :] = jnp.broadcast_to(jnp.sum(place, axis=0, keepdims=True), (8, ROWS))


def slots(leave, owner):
    return pl.pallas_call(
        slots_kernel,
        in_specs=[VMEM, VMEM],
        out_specs=[VMEM, VMEM],
        out_shape=[shape_of((24, ROWS), F32), shape_of((2, ROWS, LANES), F32)],
        compiler_params=PARAMS,
        cost_estimate=cost(3.2),
        name="slots",
    )(leave, owner)


def placed(col, arrived, stay):
    moved = jnp.dot(spreader(col, CAP), arrived, preferred_element_type=F32).astype(BF16)
    leaves = jnp.concatenate([col] * (HALF // LANES), axis=1) >= 0.0
    return jnp.where(leaves, moved.astype(F32), stay.astype(F32)).astype(BF16)


def swap_kernel(row_ref, col_ref, rows_ref, arrived_ref, next_ref, packed_ref):
    arrived = arrived_ref[...]
    for t in range(ROWS // 256):
        here = slice(t * 256, (t + 1) * 256)
        next_ref[here, :] = placed(col_ref[0, here, :], arrived, rows_ref[here, :])
    row = row_ref[8:16, :]
    for t in range(CAP // 256):
        hot = picker(row, t * 256, 256)
        packed_ref[t * 256 : (t + 1) * 256, :] = jnp.dot(hot, next_ref[...], preferred_element_type=F32).astype(BF16)


def swap(row, col, rows, arrived, half):
    whole = lambda shape: pl.BlockSpec(shape, lambda i: (0,) * len(shape))
    return pl.pallas_call(
        swap_kernel,
        grid=(1,),
        in_specs=[
            whole((24, ROWS)),
            whole((1, ROWS, LANES)),
            pl.BlockSpec((ROWS, HALF), lambda i: (0, half)),
            whole((CAP, HALF)),
        ],
        out_specs=[whole((ROWS, HALF)), whole((CAP, HALF))],
        out_shape=[shape_of((ROWS, HALF), BF16), shape_of((CAP, HALF), BF16)],
        compiler_params=PARAMS,
        cost_estimate=cost(20.0 if half == 0 else 5.3),
        name="swap",
    )(row, col, rows, arrived)


def leaf_kernel(row_ref, col_ref, rows_ref, arrived_ref, out_ref, last_ref):
    arrived = arrived_ref[...]
    for t in range(ROWS // 256):
        here = slice(t * 256, (t + 1) * 256)
        last_ref[here, :] = placed(col_ref[0, here, :], arrived, rows_ref[here, :])
    row = row_ref[16:24, :]
    for t in range(N_BLK * CAPP // 256):
        hot = picker(row, t * 256, 256)
        out_ref[t * 256 : (t + 1) * 256, :] = jnp.dot(hot, last_ref[...], preferred_element_type=F32).astype(BF16)


def leaf_pack(row, col, rows, arrived):
    whole = lambda shape: pl.BlockSpec(shape, lambda i: (0,) * len(shape))
    return pl.pallas_call(
        leaf_kernel,
        grid=(1,),
        in_specs=[
            whole((24, ROWS)),
            pl.BlockSpec((1, ROWS, LANES), lambda i: (1, 0, 0)),
            whole((ROWS, HALF)),
            whole((CAP, HALF)),
        ],
        out_specs=whole((N_BLK * CAPP, HALF)),
        out_shape=shape_of((N_BLK * CAPP, HALF), BF16),
        scratch_shapes=[pltpu.VMEM((ROWS, HALF), BF16)],
        compiler_params=PARAMS,
        cost_estimate=cost(9.8),
        name="leaf_pack",
    )(row, col, rows, arrived)


def gram_kernel(flip_ref, leave_ref, rows_ref, keep_ref, send_ref, turned_ref, masked_ref):
    turned_ref[...] = rows_ref[...].T
    flag = jnp.bitwise_xor(jnp.broadcast_to(leave_ref[0:1, :], (8, ROWS)), flip_ref[0]).astype(F32)
    lane = iota((8, LANES), 1)
    sub = iota((8, LANES), 0)
    for out_ref, weight in ((keep_ref, flag), (send_ref, 1.0 - flag)):
        masked_ref[...] = turned_ref[...] * weight[0:1, :].astype(BF16)
        sums = jnp.dot(weight.astype(BF16), rows_ref[...], preferred_element_type=F32)
        for r in range(4):
            strip = jnp.dot(
                masked_ref[r * 256 : (r + 1) * 256, :], rows_ref[:, r * 256 :], preferred_element_type=F32
            )
            for i in (2 * r, 2 * r + 1):
                for j in range(i, 8):
                    at = BLOCKS.index((i, j))
                    top = (at % 9) * LANES
                    out_ref[at // 9, top : top + LANES, :] = strip[
                        (i - 2 * r) * LANES : (i - 2 * r + 1) * LANES, (j - 2 * r) * LANES : (j - 2 * r + 1) * LANES
                    ]
        for i in range(8):
            at = BLOCKS.index((i, i))
            top = (at % 9) * LANES + 120
            own = sums[:, i * LANES : (i + 1) * LANES]
            held = jnp.where((sub == 7) & (lane < 64), own, out_ref[at // 9, top : top + 8, :])
            out_ref[at // 9, top : top + 8, :] = jnp.where((sub == 6) & (lane < 64), pltpu.roll(own, 64, 1), held)


def gram(flip, leave, rows):
    return pl.pallas_call(
        gram_kernel,
        in_specs=[SMEM, VMEM, VMEM],
        out_specs=[VMEM, VMEM],
        out_shape=[shape_of((4, CHUNK, LANES), F32)] * 2,
        scratch_shapes=[pltpu.VMEM((D, ROWS), BF16)] * 2,
        compiler_params=PARAMS,
        cost_estimate=cost(8.6),
        name="gram",
    )(flip, leave, rows)


def power_kernel(place_ref, members_ref, start_ref, a_ref, b_ref, c_ref, d_ref, out_ref, packed_ref, mat_ref):
    y, z = place_ref[0], place_ref[1]
    for k, part_ref in enumerate((a_ref, b_ref, c_ref, d_ref)):
        for m in range(4):
            at = (lax.rem(y + m, 4) * 4 + lax.rem(z + k, 4)) * PIECE
            packed_ref[pl.ds(pl.multiple_of(at, 8), PIECE), :] = part_ref[m]
    members = members_ref[0]
    lane = iota((8, LANES), 1)
    wide_lane, wide_sub = iota((LANES, LANES), 1), iota((LANES, LANES), 0)
    sums_row, sums_col = [], []
    for i in range(8):
        top = BLOCKS.index((i, i)) * LANES
        tail = packed_ref[top + 120 : top + 128, :]
        row = jnp.where(lane[0:1] < 64, tail[7:8, :], pltpu.roll(tail, 64, 1)[6:7, :])
        sums_row.append(row)
        sums_col.append(jnp.broadcast_to(row, (LANES, LANES)).T)
    for i in range(8):
        for j in range(i, 8):
            top = BLOCKS.index((i, j)) * LANES
            block = packed_ref[top : top + LANES, :]
            other = block.T
            if i == j:
                block = jnp.where((wide_sub >= 126) & (wide_lane < 64), other, block)
            hi, hj = slice(i * LANES, (i + 1) * LANES), slice(j * LANES, (j + 1) * LANES)
            mat_ref[hi, hj] = block - sums_col[i] * (sums_row[j] / members)
            if i != j:
                mat_ref[hj, hi] = other - sums_col[j] * (sums_row[i] / members)
    start = start_ref[...]
    vec = start / jnp.sqrt(jnp.sum(start * start, axis=1, keepdims=True))
    for _ in range(ITERS // 2):
        cols = []
        square = jnp.zeros((8, 1), F32)
        for i in range(8):
            total = jnp.zeros((LANES, LANES), F32)
            for j in range(8):
                total = total + mat_ref[i * LANES : (i + 1) * LANES, j * LANES : (j + 1) * LANES] * vec[
                    :, j * LANES : (j + 1) * LANES
                ]
            col = jnp.sum(total, axis=1, keepdims=True)
            cols.append(col)
        norm = sum(jnp.sum(col * col, axis=0, keepdims=True) for col in cols)
        norm = jnp.sqrt(norm)
        total = jnp.zeros((8, D), F32)
        for i in range(8):
            col = cols[i] / norm
            for s in range(LANES // 8):
                at = i * LANES + s * 8
                total = total + mat_ref[at : at + 8, :] * col[s * 8 : (s + 1) * 8, :]
        vec = jnp.sum(total, axis=0, keepdims=True)
        vec = vec / jnp.sqrt(jnp.sum(vec * vec, axis=1, keepdims=True))
    sums = jnp.concatenate(sums_row, axis=1)
    offset = jnp.sum(sums * vec, axis=1, keepdims=True) / members
    out_ref[0:8, :] = jnp.where(iota((8, D), 0) == 0, vec, offset)


def power(place, members, start, parts):
    return pl.pallas_call(
        power_kernel,
        in_specs=[SMEM, SMEM, VMEM] + [VMEM] * 4,
        out_specs=VMEM,
        out_shape=shape_of((8, D), F32),
        scratch_shapes=[pltpu.VMEM((len(BLOCKS) * LANES, LANES), F32), pltpu.VMEM((D, D), F32)],
        compiler_params=PARAMS,
        cost_estimate=cost(6.6),
        name="power",
    )(place, members, start, *parts)


def project(vec, blocks):
    sub = None
    total = None
    at = 0
    for block in blocks:
        here = vec[:, at : at + block.shape[1]]
        at += block.shape[1]
        high = here.astype(BF16)
        rest = here - high.astype(F32)
        mid = rest.astype(BF16)
        low = (rest - mid.astype(F32)).astype(BF16)
        sub = iota((8, here.shape[1]), 0)
        terms = jnp.where(
            sub == 0,
            high.astype(F32),
            jnp.where(sub == 1, mid.astype(F32), jnp.where(sub == 2, low.astype(F32), 0.0)),
        ).astype(BF16)
        part = lax.dot_general(terms, block, (((1,), (1,)), ((), ())), preferred_element_type=F32)
        total = part if total is None else total + part
    return total[0:1, :] + total[1:2, :] + total[2:3, :]


def scores_kernel(flags_ref, own_ref, core_ref, z_ref, both_ref, rows_ref, left_ref, right_ref, out_ref):
    worker = flags_ref[0] == flags_ref[1]
    same = jnp.where(worker, own_ref[...], core_ref[...])
    unlike = jnp.where(worker, both_ref[...], z_ref[...])
    even = flags_ref[1] == 0
    top = jnp.where(even, same, unlike)
    low = jnp.where(even, unlike, same)
    out_ref[0:1, :] = project(top[0:1, :], [rows_ref[...]]) - top[1:2, 0:1]
    out_ref[1:2, :] = project(low[0:1, :], [left_ref[...], right_ref[...]]) - low[1:2, 0:1]


def all_scores(flags, found, rows, left, right):
    return pl.pallas_call(
        scores_kernel,
        in_specs=[SMEM] + [VMEM] * 7,
        out_specs=VMEM,
        out_shape=shape_of((2, ROWS), F32),
        compiler_params=PARAMS,
        cost_estimate=cost(5.2),
        name="scores",
    )(flags, *found, rows, left, right)


def join_first_kernel(part_ref, out_ref):
    out_ref[...] = part_ref[...]


def join_second_kernel(part_ref, held_ref, out_ref):
    out_ref[...] = part_ref[...]


JOIN = 1024


def join_first(left):
    return pl.pallas_call(
        join_first_kernel,
        grid=(N_BLK * CAPP // JOIN,),
        in_specs=[pl.BlockSpec((JOIN, HALF), lambda i: (i, 0))],
        out_specs=pl.BlockSpec((JOIN, HALF), lambda i: (i, 0)),
        out_shape=shape_of((N_BLK * CAPP, D), BF16),
        compiler_params=PARAMS,
        cost_estimate=cost(5.2),
        name="join_first",
    )(left)


def join_second(right, held):
    return pl.pallas_call(
        join_second_kernel,
        grid=(N_BLK * CAPP // JOIN,),
        in_specs=[pl.BlockSpec((JOIN, HALF), lambda i: (i, 0)), ANY],
        out_specs=pl.BlockSpec((JOIN, HALF), lambda i: (i, 1)),
        out_shape=shape_of((N_BLK * CAPP, D), BF16),
        input_output_aliases={1: 0},
        compiler_params=PARAMS,
        cost_estimate=cost(5.2),
        name="join_second",
    )(right, held)


def along_y(value, k):
    return lax.ppermute(value, "blk", [(i, (i // 4 + k) % 4 * 4 + i % 4) for i in range(N_BLK)])


def along_z(value, k):
    return lax.ppermute(value, "cube", [(i, (i // 2 + k) % 4 * 2 + i % 2) for i in range(N_CUBE)])


def along_x(value, k):
    pairs = []
    for i in range(N_CUBE * N_BLK):
        cube, blk = i // N_BLK, i % N_BLK
        x = (blk // 2 % 2 * 2 + cube % 2 + k) % 4
        pairs.append((i, (cube // 2 * 2 + x % 2) * N_BLK + blk // 4 * 4 + x // 2 * 2 + blk % 2))
    return lax.ppermute(value, ("cube", "blk"), pairs)


def across(value, axis, bit):
    return lax.ppermute(value, axis, [(i, i ^ bit) for i in range(lax.axis_size(axis))])


def device(z, x_lo, y, x_hi, core):
    return (z * 2 + x_lo) * N_BLK + y * 4 + x_hi * 2 + core


PLACES = [(z, x_lo, y, x_hi, c) for z in range(4) for x_lo in (0, 1) for y in range(4) for x_hi in (0, 1) for c in (0, 1)]


def to_worker(value, k):
    pairs = [(device((p[0] + k) % 4, *p[1:]), device(*p)) for p in PLACES if p[0] % 2 == p[4]]
    return lax.ppermute(value, ("cube", "blk"), pairs)


def from_worker(value, dz, dc):
    pairs = [(device(*p), device(p[0] ^ dz, *p[1:4], p[4] ^ dc)) for p in PLACES if p[0] % 2 == p[4]]
    return lax.ppermute(value, ("cube", "blk"), pairs)


def after(value, earlier):
    return lax.optimization_barrier((value, earlier))[0]


def per_device(rows, start_vec, leave, owner):
    cube, blk = lax.axis_index("cube"), lax.axis_index("blk")
    z, x_lo = cube // 2, cube % 2
    y, core = blk // 4, blk % 2

    packed_l = pack_first(leave, rows, 0)
    arrived_l = across(packed_l, "cube", 1)
    leave_b = after(leave, packed_l)
    packed_r = pack_first(leave_b, rows, 1)
    row, col = slots(leave_b, owner.reshape(1, ROWS))

    flip = jnp.bitwise_xor(x_lo, core).astype(jnp.int32).reshape(1)
    leave_c, packed_r, row = lax.optimization_barrier((leave, packed_r, row))
    keep, send = gram(flip, leave_c, rows)
    got = across(send, "blk", 1)

    packed_r, arrived_l, keep = lax.optimization_barrier((packed_r, arrived_l, keep))
    arrived_r = across(packed_r, "cube", 1)
    next_l, packed_l = swap(row, col, rows, arrived_l, 0)
    arrived2_l = across(packed_l, "cube", 2)

    got = after(got, packed_l)

    def part(k):
        at = (y + k) % 4
        return lax.dynamic_index_in_dim(keep, at, 0, False) + lax.dynamic_index_in_dim(got, at, 0, False)

    parts = lax.optimization_barrier([part(k) for k in range(4)])
    moved = [along_y(parts[k], k) for k in (1, 2, 3)]

    next_r, packed_r = swap(row, col, rows, after(arrived_r, parts), 1)
    arrived2_r = across(packed_r, "cube", 2)
    leaf_l = leaf_pack(row, col, next_l, after(arrived2_l, packed_r))

    moved, _, arrived2_r = lax.optimization_barrier((moved, leaf_l, arrived2_r))
    out_l = lax.all_to_all(leaf_l, "blk", split_axis=0, concat_axis=0, tiled=True)
    own = parts[0] + moved[0] + moved[1] + moved[2]
    quarters = own.reshape(4, PIECE, LANES)
    parts = lax.optimization_barrier(
        [lax.dynamic_index_in_dim(quarters, (z + k) % 4, 0, False) for k in range(4)]
    )
    moved = [along_z(parts[k], k) for k in (1, 2, 3)]

    leaf_r = leaf_pack(row, col, next_r, after(arrived2_r, parts))

    moved = after(moved, leaf_r)
    own = parts[0] + moved[0] + moved[1] + moved[2]
    other = across(own, "blk", 1)
    both = own + other
    mine = jnp.where(core == 0, both, jnp.where(x_lo == 0, own, other))
    theirs = jnp.where(core == 0, both, jnp.where(x_lo == 0, other, own))
    piece = mine + along_x(mine, 2) + along_x(theirs, 1) + along_x(theirs, 3)
    near = [along_y(piece, -k) for k in (2, 1, 3)]
    leaf_r, near, out_l = lax.optimization_barrier((leaf_r, near, out_l))
    out_r = lax.all_to_all(leaf_r, "blk", split_axis=0, concat_axis=0, tiled=True)
    stack = jnp.stack([piece, near[1], near[0], near[2]])
    gathered = [stack] + [to_worker(stack, k) for k in (1, 2, 3)]
    held = join_first(after(out_l, stack))
    held, gathered = lax.optimization_barrier((held, gathered))

    place = jnp.stack([y, z]).astype(jnp.int32)
    members = jnp.where(core == 0, ROWS * N_BLK * N_CUBE, ROWS * N_BLK * N_CUBE // 2).astype(F32).reshape(1)
    found = power(place, members, start_vec.reshape(1, D), gathered)
    found = [found] + [from_worker(found, dz, dc) for dz, dc in ((0, 1), (1, 0), (1, 1))]
    flags = jnp.stack([core, z % 2]).astype(jnp.int32)
    scores = all_scores(flags, found, rows, next_l, next_r)
    return scores, join_second(out_r, held)


def solution(mesh):
    placed_at = (P(("cube", "blk"), None), P(), P(None, ("cube", "blk")), P(("cube", "blk"), None))
    return jax.shard_map(
        per_device,
        mesh=mesh,
        in_specs=placed_at,
        out_specs=(P(None, ("cube", "blk")), P(("cube", "blk"), None)),
        check_vma=False,
    )
```

```python
import jax
import jax.numpy as jnp
from jax import lax
from jax.experimental import pallas as pl
from jax.experimental.pallas import tpu as pltpu
from jax.sharding import PartitionSpec as P

D = 1024
ROWS = 1536
CAP = 768
CAPP = 192
N_BLK = 16
N_CUBE = 8
ITERS = 8
HALF = 512
LANES = 128
BLOCKS = [(i, j) for i in range(8) for j in range(i, 8)]
CHUNK = 9 * LANES
PIECE = CHUNK // 4
F32 = jnp.float32
BF16 = jnp.bfloat16


def params(mebibytes):
    return pltpu.CompilerParams(vmem_limit_bytes=mebibytes * 2**20)


def cost(microseconds):
    return pl.CostEstimate(
        flops=int(microseconds * 1.15e9), bytes_accessed=int(microseconds * 3.69e6), transcendentals=0
    )


VMEM = pl.BlockSpec(memory_space=pltpu.VMEM)
SMEM = pl.BlockSpec(memory_space=pltpu.SMEM)
ANY = pl.BlockSpec(memory_space=pl.ANY)


def iota(shape, dim):
    return lax.broadcasted_iota(jnp.int32, shape, dim)


def shape_of(shape, dtype):
    return jax.ShapeDtypeStruct(shape, dtype)


def running_count(flags):
    upper = jnp.where(iota((LANES, LANES), 0) <= iota((LANES, LANES), 1), 1.0, 0.0).astype(BF16)
    parts = []
    before = jnp.zeros((flags.shape[0], 1), F32)
    for b in range(ROWS // LANES):
        part = flags[:, b * LANES : (b + 1) * LANES].astype(BF16)
        part = jnp.dot(part, upper, preferred_element_type=F32) + before
        before = part[:, LANES - 1 : LANES]
        parts.append(part)
    return jnp.concatenate(parts, axis=1)


def slot_row(leave_ref, level):
    flags = jnp.broadcast_to(leave_ref[level : level + 1, :].astype(F32), (8, ROWS))
    return jnp.where(flags > 0.5, running_count(flags) - 1.0, -1.0)


def store_column(row, col_ref):
    for b in range(ROWS // LANES):
        part = jnp.broadcast_to(row[0:1, b * LANES : (b + 1) * LANES], (LANES, LANES))
        col_ref[b * LANES : (b + 1) * LANES, :] = part.T


def picker(row, first, count):
    slots = (iota((count, ROWS), 0) + first).astype(F32)
    return jnp.where(slots == row[0:1, :], 1.0, 0.0).astype(BF16)


def spreader(col, slots):
    parts = []
    for t in range(slots // LANES):
        lanes = (iota(col.shape, 1) + t * LANES).astype(F32)
        parts.append(jnp.where(col == lanes, 1.0, 0.0).astype(BF16))
    return jnp.concatenate(parts, axis=1)


def pack_first_kernel(leave_ref, rows_ref, out_ref):
    row = slot_row(leave_ref, 0)
    for t in range(CAP // 256):
        hot = picker(row, t * 256, 256)
        out_ref[t * 256 : (t + 1) * 256, :] = jnp.dot(hot, rows_ref[...], preferred_element_type=F32).astype(BF16)


def pack_first(leave, rows, half):
    return pl.pallas_call(
        pack_first_kernel,
        grid=(1,),
        in_specs=[pl.BlockSpec((2, ROWS), lambda i: (0, 0)), pl.BlockSpec((ROWS, HALF), lambda i: (0, half))],
        out_specs=pl.BlockSpec((CAP, HALF), lambda i: (0, 0)),
        out_shape=shape_of((CAP, HALF), BF16),
        compiler_params=params(8),
        cost_estimate=cost(4.3),
        name="pack_first",
    )(leave, in_hbm(rows))


def slots_kernel(leave_ref, owner_ref, row_ref):
    for level in range(2):
        row_ref[level * 8 : (level + 1) * 8, :] = slot_row(leave_ref, level)
    owner = jnp.broadcast_to(owner_ref[...], (N_BLK, ROWS))
    named = jnp.where(owner == iota((N_BLK, ROWS), 0), 1.0, 0.0)
    place = named * (running_count(named) - 1.0 + (iota((N_BLK, ROWS), 0) * CAPP).astype(F32))
    row_ref[16:24, :] = jnp.broadcast_to(jnp.sum(place, axis=0, keepdims=True), (8, ROWS))


def slots(leave, owner):
    return pl.pallas_call(
        slots_kernel,
        in_specs=[VMEM, VMEM],
        out_specs=VMEM,
        out_shape=shape_of((24, ROWS), F32),
        compiler_params=params(6),
        cost_estimate=cost(3.2),
        name="slots",
    )(leave, owner)


def in_hbm(value):
    return pltpu.with_memory_space_constraint(value, pltpu.HBM)


def placed(col, arrived, stay):
    moved = jnp.dot(spreader(col, CAP), arrived, preferred_element_type=F32).astype(BF16)
    leaves = jnp.concatenate([col] * (HALF // LANES), axis=1) >= 0.0
    return jnp.where(leaves, moved.astype(F32), stay.astype(F32)).astype(BF16)


def whole(shape):
    return pl.BlockSpec(shape, lambda i: (0,) * len(shape))


def swap_kernel(row_ref, rows_ref, arrived_ref, next_ref, packed_ref, col_ref):
    store_column(row_ref[0:8, :], col_ref)
    arrived = arrived_ref[...]
    for t in range(ROWS // 256):
        here = slice(t * 256, (t + 1) * 256)
        next_ref[here, :] = placed(col_ref[here, :], arrived, rows_ref[here, :])
    row = row_ref[8:16, :]
    for t in range(CAP // 256):
        hot = picker(row, t * 256, 256)
        packed_ref[t * 256 : (t + 1) * 256, :] = jnp.dot(hot, next_ref[...], preferred_element_type=F32).astype(BF16)


def swap(row, rows, arrived, half):
    return pl.pallas_call(
        swap_kernel,
        grid=(1,),
        in_specs=[whole((24, ROWS)), pl.BlockSpec((ROWS, HALF), lambda i: (0, half)), whole((CAP, HALF))],
        out_specs=[whole((ROWS, HALF)), whole((CAP, HALF))],
        out_shape=[shape_of((ROWS, HALF), BF16), shape_of((CAP, HALF), BF16)],
        scratch_shapes=[pltpu.VMEM((ROWS, LANES), F32)],
        compiler_params=params(12),
        cost_estimate=cost(20.0 if half == 0 else 5.3),
        name="swap",
    )(row, in_hbm(rows), arrived)


SLOTS = 768


def leaf_kernel(row_ref, rows_ref, arrived_ref, out_ref, last_ref, col_ref):
    @pl.when(pl.program_id(0) == 0)
    def _():
        store_column(row_ref[8:16, :], col_ref)
        arrived = arrived_ref[...]
        for t in range(ROWS // 256):
            here = slice(t * 256, (t + 1) * 256)
            last_ref[here, :] = placed(col_ref[here, :], arrived, rows_ref[here, :])

    row = row_ref[16:24, :] - (pl.program_id(0) * SLOTS).astype(F32)
    for t in range(SLOTS // 256):
        hot = picker(row, t * 256, 256)
        out_ref[t * 256 : (t + 1) * 256, :] = jnp.dot(hot, last_ref[...], preferred_element_type=F32).astype(BF16)


def leaf_pack(row, rows, arrived):
    return pl.pallas_call(
        leaf_kernel,
        grid=(N_BLK * CAPP // SLOTS,),
        in_specs=[whole((24, ROWS)), whole((ROWS, HALF)), whole((CAP, HALF))],
        out_specs=pl.BlockSpec((SLOTS, HALF), lambda i: (i, 0)),
        out_shape=pltpu.HBM((N_BLK * CAPP, HALF), BF16),
        scratch_shapes=[pltpu.VMEM((ROWS, HALF), BF16), pltpu.VMEM((ROWS, LANES), F32)],
        compiler_params=params(16),
        cost_estimate=cost(9.8),
        name="leaf_pack",
    )(row, rows, arrived)


def gram_kernel(flip_ref, leave_ref, rows_ref, keep_ref, send_ref, turned_ref, masked_ref):
    turned_ref[...] = rows_ref[...].T
    flag = jnp.bitwise_xor(jnp.broadcast_to(leave_ref[0:1, :], (8, ROWS)), flip_ref[0]).astype(F32)
    lane = iota((8, LANES), 1)
    sub = iota((8, LANES), 0)
    for out_ref, weight in ((keep_ref, flag), (send_ref, 1.0 - flag)):
        masked_ref[...] = turned_ref[...] * weight[0:1, :].astype(BF16)
        sums = jnp.dot(weight.astype(BF16), rows_ref[...], preferred_element_type=F32)
        for r in range(4):
            strip = jnp.dot(
                masked_ref[r * 256 : (r + 1) * 256, :], rows_ref[:, r * 256 :], preferred_element_type=F32
            )
            for i in (2 * r, 2 * r + 1):
                for j in range(i, 8):
                    at = BLOCKS.index((i, j))
                    top = (at % 9) * LANES
                    out_ref[at // 9, top : top + LANES, :] = strip[
                        (i - 2 * r) * LANES : (i - 2 * r + 1) * LANES, (j - 2 * r) * LANES : (j - 2 * r + 1) * LANES
                    ]
        for i in range(8):
            at = BLOCKS.index((i, i))
            top = (at % 9) * LANES + 120
            own = sums[:, i * LANES : (i + 1) * LANES]
            held = jnp.where((sub == 7) & (lane < 64), own, out_ref[at // 9, top : top + 8, :])
            out_ref[at // 9, top : top + 8, :] = jnp.where((sub == 6) & (lane < 64), pltpu.roll(own, 64, 1), held)


def gram(flip, leave, rows):
    return pl.pallas_call(
        gram_kernel,
        in_specs=[SMEM, VMEM, VMEM],
        out_specs=[VMEM, VMEM],
        out_shape=[shape_of((4, CHUNK, LANES), F32)] * 2,
        scratch_shapes=[pltpu.VMEM((D, ROWS), BF16)] * 2,
        compiler_params=params(22),
        cost_estimate=cost(8.6),
        name="gram",
    )(flip, leave, rows)


def power_kernel(place_ref, members_ref, start_ref, a_ref, b_ref, c_ref, d_ref, out_ref, packed_ref, mat_ref):
    y, z = place_ref[0], place_ref[1]
    for k, part_ref in enumerate((a_ref, b_ref, c_ref, d_ref)):
        for m in range(4):
            at = (lax.rem(y + m, 4) * 4 + lax.rem(z + k, 4)) * PIECE
            packed_ref[pl.ds(pl.multiple_of(at, 8), PIECE), :] = part_ref[m]
    members = members_ref[0]
    lane = iota((8, LANES), 1)
    wide_lane, wide_sub = iota((LANES, LANES), 1), iota((LANES, LANES), 0)
    sums_row, sums_col = [], []
    for i in range(8):
        top = BLOCKS.index((i, i)) * LANES
        tail = packed_ref[top + 120 : top + 128, :]
        row = jnp.where(lane[0:1] < 64, tail[7:8, :], pltpu.roll(tail, 64, 1)[6:7, :])
        sums_row.append(row)
        sums_col.append(jnp.broadcast_to(row, (LANES, LANES)).T)
    for i in range(8):
        for j in range(i, 8):
            top = BLOCKS.index((i, j)) * LANES
            block = packed_ref[top : top + LANES, :]
            other = block.T
            if i == j:
                block = jnp.where((wide_sub >= 126) & (wide_lane < 64), other, block)
            hi, hj = slice(i * LANES, (i + 1) * LANES), slice(j * LANES, (j + 1) * LANES)
            mat_ref[hi, hj] = block - sums_col[i] * (sums_row[j] / members)
            if i != j:
                mat_ref[hj, hi] = other - sums_col[j] * (sums_row[i] / members)
    start = start_ref[...]
    vec = start / jnp.sqrt(jnp.sum(start * start, axis=1, keepdims=True))
    for _ in range(ITERS // 2):
        cols = []
        square = jnp.zeros((8, 1), F32)
        for i in range(8):
            total = jnp.zeros((LANES, LANES), F32)
            for j in range(8):
                total = total + mat_ref[i * LANES : (i + 1) * LANES, j * LANES : (j + 1) * LANES] * vec[
                    :, j * LANES : (j + 1) * LANES
                ]
            col = jnp.sum(total, axis=1, keepdims=True)
            cols.append(col)
        norm = sum(jnp.sum(col * col, axis=0, keepdims=True) for col in cols)
        norm = jnp.sqrt(norm)
        total = jnp.zeros((8, D), F32)
        for i in range(8):
            col = cols[i] / norm
            for s in range(LANES // 8):
                at = i * LANES + s * 8
                total = total + mat_ref[at : at + 8, :] * col[s * 8 : (s + 1) * 8, :]
        vec = jnp.sum(total, axis=0, keepdims=True)
        vec = vec / jnp.sqrt(jnp.sum(vec * vec, axis=1, keepdims=True))
    sums = jnp.concatenate(sums_row, axis=1)
    offset = jnp.sum(sums * vec, axis=1, keepdims=True) / members
    out_ref[0:8, :] = jnp.where(iota((8, D), 0) == 0, vec, offset)


def power(place, members, start, parts):
    return pl.pallas_call(
        power_kernel,
        in_specs=[SMEM, SMEM, VMEM] + [VMEM] * 4,
        out_specs=VMEM,
        out_shape=shape_of((8, D), F32),
        scratch_shapes=[pltpu.VMEM((len(BLOCKS) * LANES, LANES), F32), pltpu.VMEM((D, D), F32)],
        compiler_params=params(12),
        cost_estimate=cost(6.6),
        name="power",
    )(place, members, start, *parts)


def project(vec, blocks):
    sub = None
    total = None
    at = 0
    for block in blocks:
        here = vec[:, at : at + block.shape[1]]
        at += block.shape[1]
        high = here.astype(BF16)
        rest = here - high.astype(F32)
        mid = rest.astype(BF16)
        low = (rest - mid.astype(F32)).astype(BF16)
        sub = iota((8, here.shape[1]), 0)
        terms = jnp.where(
            sub == 0,
            high.astype(F32),
            jnp.where(sub == 1, mid.astype(F32), jnp.where(sub == 2, low.astype(F32), 0.0)),
        ).astype(BF16)
        part = lax.dot_general(terms, block, (((1,), (1,)), ((), ())), preferred_element_type=F32)
        total = part if total is None else total + part
    return total[0:1, :] + total[1:2, :] + total[2:3, :]


def scores_kernel(flags_ref, own_ref, core_ref, z_ref, both_ref, rows_ref, left_ref, right_ref, out_ref):
    worker = flags_ref[0] == flags_ref[1]
    same = jnp.where(worker, own_ref[...], core_ref[...])
    unlike = jnp.where(worker, both_ref[...], z_ref[...])
    even = flags_ref[1] == 0
    top = jnp.where(even, same, unlike)
    low = jnp.where(even, unlike, same)
    out_ref[0:1, :] = project(top[0:1, :], [rows_ref[...]]) - top[1:2, 0:1]
    out_ref[1:2, :] = project(low[0:1, :], [left_ref[...], right_ref[...]]) - low[1:2, 0:1]


def all_scores(flags, found, rows, left, right):
    return pl.pallas_call(
        scores_kernel,
        in_specs=[SMEM] + [VMEM] * 7,
        out_specs=VMEM,
        out_shape=shape_of((2, ROWS), F32),
        compiler_params=params(8),
        cost_estimate=cost(5.2),
        name="scores",
    )(flags, *found, rows, left, right)


def join_first_kernel(part_ref, out_ref):
    out_ref[...] = part_ref[...]


def join_second_kernel(part_ref, held_ref, out_ref):
    out_ref[...] = part_ref[...]


JOIN = 1024


def join_first(left):
    return pl.pallas_call(
        join_first_kernel,
        grid=(N_BLK * CAPP // JOIN,),
        in_specs=[pl.BlockSpec((JOIN, HALF), lambda i: (i, 0))],
        out_specs=pl.BlockSpec((JOIN, HALF), lambda i: (i, 0)),
        out_shape=shape_of((N_BLK * CAPP, D), BF16),
        compiler_params=params(10),
        cost_estimate=cost(5.2),
        name="join_first",
    )(left)


def join_second(right, held):
    return pl.pallas_call(
        join_second_kernel,
        grid=(N_BLK * CAPP // JOIN,),
        in_specs=[pl.BlockSpec((JOIN, HALF), lambda i: (i, 0)), ANY],
        out_specs=pl.BlockSpec((JOIN, HALF), lambda i: (i, 1)),
        out_shape=shape_of((N_BLK * CAPP, D), BF16),
        input_output_aliases={1: 0},
        compiler_params=params(10),
        cost_estimate=cost(5.2),
        name="join_second",
    )(right, held)


def along_y(value, k):
    return lax.ppermute(value, "blk", [(i, (i // 4 + k) % 4 * 4 + i % 4) for i in range(N_BLK)])


def along_z(value, k):
    return lax.ppermute(value, "cube", [(i, (i // 2 + k) % 4 * 2 + i % 2) for i in range(N_CUBE)])


def along_x(value, k):
    pairs = []
    for i in range(N_CUBE * N_BLK):
        cube, blk = i // N_BLK, i % N_BLK
        x = (blk // 2 % 2 * 2 + cube % 2 + k) % 4
        pairs.append((i, (cube // 2 * 2 + x % 2) * N_BLK + blk // 4 * 4 + x // 2 * 2 + blk % 2))
    return lax.ppermute(value, ("cube", "blk"), pairs)


def across(value, axis, bit):
    return lax.ppermute(value, axis, [(i, i ^ bit) for i in range(lax.axis_size(axis))])


def device(z, x_lo, y, x_hi, core):
    return (z * 2 + x_lo) * N_BLK + y * 4 + x_hi * 2 + core


PLACES = [(z, x_lo, y, x_hi, c) for z in range(4) for x_lo in (0, 1) for y in range(4) for x_hi in (0, 1) for c in (0, 1)]


def to_worker(value, k):
    pairs = [(device((p[0] + k) % 4, *p[1:]), device(*p)) for p in PLACES if p[0] % 2 == p[4]]
    return lax.ppermute(value, ("cube", "blk"), pairs)


def from_worker(value, dz, dc):
    pairs = [(device(*p), device(p[0] ^ dz, *p[1:4], p[4] ^ dc)) for p in PLACES if p[0] % 2 == p[4]]
    return lax.ppermute(value, ("cube", "blk"), pairs)


def after(value, earlier):
    return lax.optimization_barrier((value, earlier))[0]


def per_device(rows, start_vec, leave, owner):
    cube, blk = lax.axis_index("cube"), lax.axis_index("blk")
    z, x_lo = cube // 2, cube % 2
    y, core = blk // 4, blk % 2

    packed_l = pack_first(leave, rows, 0)
    arrived_l = across(packed_l, "cube", 1)
    leave_b = after(leave, packed_l)
    packed_r = pack_first(leave_b, rows, 1)
    row = slots(leave_b, owner.reshape(1, ROWS))

    flip = jnp.bitwise_xor(x_lo, core).astype(jnp.int32).reshape(1)
    leave_c, packed_r, row = lax.optimization_barrier((leave, packed_r, row))
    keep, send = gram(flip, leave_c, rows)
    got = across(send, "blk", 1)

    packed_r, arrived_l, keep = lax.optimization_barrier((packed_r, arrived_l, keep))
    arrived_r = across(packed_r, "cube", 1)
    next_l, packed_l = swap(row, rows, arrived_l, 0)
    arrived2_l = across(packed_l, "cube", 2)

    got = after(got, packed_l)

    def part(k):
        at = (y + k) % 4
        return lax.dynamic_index_in_dim(keep, at, 0, False) + lax.dynamic_index_in_dim(got, at, 0, False)

    parts = lax.optimization_barrier([part(k) for k in range(4)])
    moved = [along_y(parts[k], k) for k in (1, 2, 3)]

    next_r, packed_r = swap(row, rows, after(arrived_r, parts), 1)
    arrived2_r = across(packed_r, "cube", 2)
    leaf_l = leaf_pack(row, next_l, after(arrived2_l, packed_r))

    moved, _, arrived2_r = lax.optimization_barrier((moved, leaf_l, arrived2_r))
    out_l = lax.all_to_all(leaf_l, "blk", split_axis=0, concat_axis=0, tiled=True)
    own = parts[0] + moved[0] + moved[1] + moved[2]
    quarters = own.reshape(4, PIECE, LANES)
    parts = lax.optimization_barrier(
        [lax.dynamic_index_in_dim(quarters, (z + k) % 4, 0, False) for k in range(4)]
    )
    moved = [along_z(parts[k], k) for k in (1, 2, 3)]

    leaf_r = leaf_pack(row, next_r, after(arrived2_r, parts))

    moved = after(moved, leaf_r)
    own = parts[0] + moved[0] + moved[1] + moved[2]
    other = across(own, "blk", 1)
    both = own + other
    mine = jnp.where(core == 0, both, jnp.where(x_lo == 0, own, other))
    theirs = jnp.where(core == 0, both, jnp.where(x_lo == 0, other, own))
    piece = mine + along_x(mine, 2) + along_x(theirs, 1) + along_x(theirs, 3)
    near = [along_y(piece, -k) for k in (2, 1, 3)]
    leaf_r, near, out_l = lax.optimization_barrier((leaf_r, near, out_l))
    out_r = lax.all_to_all(leaf_r, "blk", split_axis=0, concat_axis=0, tiled=True)
    stack = jnp.stack([piece, near[1], near[0], near[2]])
    gathered = [stack] + [to_worker(stack, k) for k in (1, 2, 3)]
    held = join_first(after(out_l, stack))
    held, gathered = lax.optimization_barrier((held, gathered))

    place = jnp.stack([y, z]).astype(jnp.int32)
    members = jnp.where(core == 0, ROWS * N_BLK * N_CUBE, ROWS * N_BLK * N_CUBE // 2).astype(F32).reshape(1)
    found = power(place, members, start_vec.reshape(1, D), gathered)
    found = [found] + [from_worker(found, dz, dc) for dz, dc in ((0, 1), (1, 0), (1, 1))]
    flags = jnp.stack([core, z % 2]).astype(jnp.int32)
    scores = all_scores(flags, found, rows, next_l, next_r)
    return scores, join_second(out_r, held)


def solution(mesh):
    placed_at = (P(("cube", "blk"), None), P(), P(None, ("cube", "blk")), P(("cube", "blk"), None))
    return jax.shard_map(
        per_device,
        mesh=mesh,
        in_specs=placed_at,
        out_specs=(P(None, ("cube", "blk")), P(("cube", "blk"), None)),
        check_vma=False,
    )
```

```python
import jax
import jax.numpy as jnp
from jax import lax
from jax.experimental import pallas as pl
from jax.experimental.pallas import tpu as pltpu
from jax.sharding import PartitionSpec as P

D = 1024
ROWS = 1536
CAP = 768
CAPP = 192
N_BLK = 16
N_CUBE = 8
ITERS = 8
HALF = 512
LANES = 128
BLOCKS = [(i, j) for i in range(8) for j in range(i, 8)]
CHUNK = 9 * LANES
PIECE = CHUNK // 4
F32 = jnp.float32
BF16 = jnp.bfloat16


def params(mebibytes):
    return pltpu.CompilerParams(vmem_limit_bytes=mebibytes * 2**20)


def cost(microseconds):
    return pl.CostEstimate(
        flops=int(microseconds * 1.15e9), bytes_accessed=int(microseconds * 3.69e6), transcendentals=0
    )


VMEM = pl.BlockSpec(memory_space=pltpu.VMEM)
SMEM = pl.BlockSpec(memory_space=pltpu.SMEM)
ANY = pl.BlockSpec(memory_space=pl.ANY)


def iota(shape, dim):
    return lax.broadcasted_iota(jnp.int32, shape, dim)


def shape_of(shape, dtype):
    return jax.ShapeDtypeStruct(shape, dtype)


def running_count(flags):
    upper = jnp.where(iota((LANES, LANES), 0) <= iota((LANES, LANES), 1), 1.0, 0.0).astype(BF16)
    parts = []
    before = jnp.zeros((flags.shape[0], 1), F32)
    for b in range(ROWS // LANES):
        part = flags[:, b * LANES : (b + 1) * LANES].astype(BF16)
        part = jnp.dot(part, upper, preferred_element_type=F32) + before
        before = part[:, LANES - 1 : LANES]
        parts.append(part)
    return jnp.concatenate(parts, axis=1)


def slot_row(leave_ref, level):
    flags = jnp.broadcast_to(leave_ref[level : level + 1, :].astype(F32), (8, ROWS))
    return jnp.where(flags > 0.5, running_count(flags) - 1.0, -1.0)


def store_column(row, col_ref):
    for b in range(ROWS // LANES):
        part = jnp.broadcast_to(row[0:1, b * LANES : (b + 1) * LANES], (LANES, LANES))
        col_ref[b * LANES : (b + 1) * LANES, :] = part.T


def picker(row, first, count):
    slots = (iota((count, ROWS), 0) + first).astype(F32)
    return jnp.where(slots == row[0:1, :], 1.0, 0.0).astype(BF16)


def spreader(col, slots):
    parts = []
    for t in range(slots // LANES):
        lanes = (iota(col.shape, 1) + t * LANES).astype(F32)
        parts.append(jnp.where(col == lanes, 1.0, 0.0).astype(BF16))
    return jnp.concatenate(parts, axis=1)


def pack_first_kernel(leave_ref, rows_ref, out_ref):
    row = slot_row(leave_ref, 0)
    for t in range(CAP // 256):
        hot = picker(row, t * 256, 256)
        out_ref[t * 256 : (t + 1) * 256, :] = jnp.dot(hot, rows_ref[...], preferred_element_type=F32).astype(BF16)


def pack_first(leave, rows, half):
    return pl.pallas_call(
        pack_first_kernel,
        grid=(1,),
        in_specs=[pl.BlockSpec((2, ROWS), lambda i: (0, 0)), pl.BlockSpec((ROWS, HALF), lambda i: (0, half))],
        out_specs=pl.BlockSpec((CAP, HALF), lambda i: (0, 0)),
        out_shape=shape_of((CAP, HALF), BF16),
        compiler_params=params(8),
        cost_estimate=cost(4.3),
        name="pack_first",
    )(leave, in_hbm(rows))


def slots_kernel(leave_ref, owner_ref, row_ref):
    for level in range(2):
        row_ref[level * 8 : (level + 1) * 8, :] = slot_row(leave_ref, level)
    owner = jnp.broadcast_to(owner_ref[...], (N_BLK, ROWS))
    named = jnp.where(owner == iota((N_BLK, ROWS), 0), 1.0, 0.0)
    place = named * (running_count(named) - 1.0 + (iota((N_BLK, ROWS), 0) * CAPP).astype(F32))
    row_ref[16:24, :] = jnp.broadcast_to(jnp.sum(place, axis=0, keepdims=True), (8, ROWS))


def slots(leave, owner):
    return pl.pallas_call(
        slots_kernel,
        in_specs=[VMEM, VMEM],
        out_specs=VMEM,
        out_shape=shape_of((24, ROWS), F32),
        compiler_params=params(6),
        cost_estimate=cost(3.2),
        name="slots",
    )(leave, owner)


def in_hbm(value):
    return pltpu.with_memory_space_constraint(value, pltpu.HBM)


def placed(col, arrived, stay):
    moved = jnp.dot(spreader(col, CAP), arrived, preferred_element_type=F32).astype(BF16)
    leaves = jnp.concatenate([col] * (HALF // LANES), axis=1) >= 0.0
    return jnp.where(leaves, moved.astype(F32), stay.astype(F32)).astype(BF16)


def whole(shape):
    return pl.BlockSpec(shape, lambda i: (0,) * len(shape))


def swap_kernel(row_ref, rows_ref, arrived_ref, next_ref, packed_ref, col_ref):
    store_column(row_ref[0:8, :], col_ref)
    arrived = arrived_ref[...]
    for t in range(ROWS // 256):
        here = slice(t * 256, (t + 1) * 256)
        next_ref[here, :] = placed(col_ref[here, :], arrived, rows_ref[here, :])
    row = row_ref[8:16, :]
    for t in range(CAP // 256):
        hot = picker(row, t * 256, 256)
        packed_ref[t * 256 : (t + 1) * 256, :] = jnp.dot(hot, next_ref[...], preferred_element_type=F32).astype(BF16)


def swap(row, rows, arrived, half):
    return pl.pallas_call(
        swap_kernel,
        grid=(1,),
        in_specs=[whole((24, ROWS)), pl.BlockSpec((ROWS, HALF), lambda i: (0, half)), whole((CAP, HALF))],
        out_specs=[whole((ROWS, HALF)), whole((CAP, HALF))],
        out_shape=[shape_of((ROWS, HALF), BF16), shape_of((CAP, HALF), BF16)],
        scratch_shapes=[pltpu.VMEM((ROWS, LANES), F32)],
        compiler_params=params(12),
        cost_estimate=cost(20.0 if half == 0 else 5.3),
        name="swap",
    )(row, in_hbm(rows), arrived)


SLOTS = 768


def leaf_kernel(row_ref, rows_ref, arrived_ref, out_ref, last_ref, col_ref):
    @pl.when(pl.program_id(0) == 0)
    def _():
        store_column(row_ref[8:16, :], col_ref)
        arrived = arrived_ref[...]
        for t in range(ROWS // 256):
            here = slice(t * 256, (t + 1) * 256)
            last_ref[here, :] = placed(col_ref[here, :], arrived, rows_ref[here, :])

    row = row_ref[16:24, :] - (pl.program_id(0) * SLOTS).astype(F32)
    for t in range(SLOTS // 256):
        hot = picker(row, t * 256, 256)
        out_ref[t * 256 : (t + 1) * 256, :] = jnp.dot(hot, last_ref[...], preferred_element_type=F32).astype(BF16)


def leaf_pack(row, rows, arrived):
    return pl.pallas_call(
        leaf_kernel,
        grid=(N_BLK * CAPP // SLOTS,),
        in_specs=[whole((24, ROWS)), whole((ROWS, HALF)), whole((CAP, HALF))],
        out_specs=pl.BlockSpec((SLOTS, HALF), lambda i: (i, 0)),
        out_shape=pltpu.HBM((N_BLK * CAPP, HALF), BF16),
        scratch_shapes=[pltpu.VMEM((ROWS, HALF), BF16), pltpu.VMEM((ROWS, LANES), F32)],
        compiler_params=params(16),
        cost_estimate=cost(9.8),
        name="leaf_pack",
    )(row, rows, arrived)


def gram_kernel(flip_ref, leave_ref, rows_ref, keep_ref, send_ref, turned_ref, masked_ref):
    turned_ref[...] = rows_ref[...].T
    flag = jnp.bitwise_xor(jnp.broadcast_to(leave_ref[0:1, :], (8, ROWS)), flip_ref[0]).astype(F32)
    lane = iota((8, LANES), 1)
    sub = iota((8, LANES), 0)
    for out_ref, weight in ((keep_ref, flag), (send_ref, 1.0 - flag)):
        masked_ref[...] = turned_ref[...] * weight[0:1, :].astype(BF16)
        sums = jnp.dot(weight.astype(BF16), rows_ref[...], preferred_element_type=F32)
        for r in range(4):
            strip = jnp.dot(
                masked_ref[r * 256 : (r + 1) * 256, :], rows_ref[:, r * 256 :], preferred_element_type=F32
            )
            for i in (2 * r, 2 * r + 1):
                for j in range(i, 8):
                    at = BLOCKS.index((i, j))
                    top = (at % 9) * LANES
                    out_ref[at // 9, top : top + LANES, :] = strip[
                        (i - 2 * r) * LANES : (i - 2 * r + 1) * LANES, (j - 2 * r) * LANES : (j - 2 * r + 1) * LANES
                    ]
        for i in range(8):
            at = BLOCKS.index((i, i))
            top = (at % 9) * LANES + 120
            own = sums[:, i * LANES : (i + 1) * LANES]
            held = jnp.where((sub == 7) & (lane < 64), own, out_ref[at // 9, top : top + 8, :])
            out_ref[at // 9, top : top + 8, :] = jnp.where((sub == 6) & (lane < 64), pltpu.roll(own, 64, 1), held)


def gram(flip, leave, rows):
    return pl.pallas_call(
        gram_kernel,
        in_specs=[SMEM, VMEM, VMEM],
        out_specs=[VMEM, VMEM],
        out_shape=[shape_of((4, CHUNK, LANES), F32)] * 2,
        scratch_shapes=[pltpu.VMEM((D, ROWS), BF16)] * 2,
        compiler_params=params(22),
        cost_estimate=cost(8.6),
        name="gram",
    )(flip, leave, rows)


def power_kernel(place_ref, members_ref, start_ref, a_ref, b_ref, c_ref, d_ref, out_ref, packed_ref, mat_ref):
    y, z = place_ref[0], place_ref[1]
    for k, part_ref in enumerate((a_ref, b_ref, c_ref, d_ref)):
        for m in range(4):
            at = (lax.rem(y + m, 4) * 4 + lax.rem(z + k, 4)) * PIECE
            packed_ref[pl.ds(pl.multiple_of(at, 8), PIECE), :] = part_ref[m]
    members = members_ref[0]
    lane = iota((8, LANES), 1)
    wide_lane, wide_sub = iota((LANES, LANES), 1), iota((LANES, LANES), 0)
    sums_row, sums_col = [], []
    for i in range(8):
        top = BLOCKS.index((i, i)) * LANES
        tail = packed_ref[top + 120 : top + 128, :]
        row = jnp.where(lane[0:1] < 64, tail[7:8, :], pltpu.roll(tail, 64, 1)[6:7, :])
        sums_row.append(row)
        sums_col.append(jnp.broadcast_to(row, (LANES, LANES)).T)
    for i in range(8):
        for j in range(i, 8):
            top = BLOCKS.index((i, j)) * LANES
            block = packed_ref[top : top + LANES, :]
            other = block.T
            if i == j:
                block = jnp.where((wide_sub >= 126) & (wide_lane < 64), other, block)
            hi, hj = slice(i * LANES, (i + 1) * LANES), slice(j * LANES, (j + 1) * LANES)
            mat_ref[hi, hj] = block - sums_col[i] * (sums_row[j] / members)
            if i != j:
                mat_ref[hj, hi] = other - sums_col[j] * (sums_row[i] / members)
    start = start_ref[...]
    vec = start / jnp.sqrt(jnp.sum(start * start, axis=1, keepdims=True))
    for _ in range(ITERS // 2):
        cols = []
        square = jnp.zeros((8, 1), F32)
        for i in range(8):
            total = jnp.zeros((LANES, LANES), F32)
            for j in range(8):
                total = total + mat_ref[i * LANES : (i + 1) * LANES, j * LANES : (j + 1) * LANES] * vec[
                    :, j * LANES : (j + 1) * LANES
                ]
            col = jnp.sum(total, axis=1, keepdims=True)
            cols.append(col)
        norm = sum(jnp.sum(col * col, axis=0, keepdims=True) for col in cols)
        norm = jnp.sqrt(norm)
        total = jnp.zeros((8, D), F32)
        for i in range(8):
            col = cols[i] / norm
            for s in range(LANES // 8):
                at = i * LANES + s * 8
                total = total + mat_ref[at : at + 8, :] * col[s * 8 : (s + 1) * 8, :]
        vec = jnp.sum(total, axis=0, keepdims=True)
        vec = vec / jnp.sqrt(jnp.sum(vec * vec, axis=1, keepdims=True))
    sums = jnp.concatenate(sums_row, axis=1)
    offset = jnp.sum(sums * vec, axis=1, keepdims=True) / members
    out_ref[0:8, :] = jnp.where(iota((8, D), 0) == 0, vec, offset)


def power(place, members, start, parts):
    return pl.pallas_call(
        power_kernel,
        in_specs=[SMEM, SMEM, VMEM] + [VMEM] * 4,
        out_specs=VMEM,
        out_shape=shape_of((8, D), F32),
        scratch_shapes=[pltpu.VMEM((len(BLOCKS) * LANES, LANES), F32), pltpu.VMEM((D, D), F32)],
        compiler_params=params(12),
        cost_estimate=cost(6.6),
        name="power",
    )(place, members, start, *parts)


def project(vec, blocks):
    sub = None
    total = None
    at = 0
    for block in blocks:
        here = vec[:, at : at + block.shape[1]]
        at += block.shape[1]
        high = here.astype(BF16)
        rest = here - high.astype(F32)
        mid = rest.astype(BF16)
        low = (rest - mid.astype(F32)).astype(BF16)
        sub = iota((8, here.shape[1]), 0)
        terms = jnp.where(
            sub == 0,
            high.astype(F32),
            jnp.where(sub == 1, mid.astype(F32), jnp.where(sub == 2, low.astype(F32), 0.0)),
        ).astype(BF16)
        part = lax.dot_general(terms, block, (((1,), (1,)), ((), ())), preferred_element_type=F32)
        total = part if total is None else total + part
    return total[0:1, :] + total[1:2, :] + total[2:3, :]


def scores_kernel(flags_ref, own_ref, core_ref, z_ref, both_ref, rows_ref, left_ref, right_ref, out_ref):
    worker = flags_ref[0] == flags_ref[1]
    same = jnp.where(worker, own_ref[...], core_ref[...])
    unlike = jnp.where(worker, both_ref[...], z_ref[...])
    even = flags_ref[1] == 0
    top = jnp.where(even, same, unlike)
    low = jnp.where(even, unlike, same)
    out_ref[0:1, :] = project(top[0:1, :], [rows_ref[...]]) - top[1:2, 0:1]
    out_ref[1:2, :] = project(low[0:1, :], [left_ref[...], right_ref[...]]) - low[1:2, 0:1]


def all_scores(flags, found, rows, left, right):
    return pl.pallas_call(
        scores_kernel,
        in_specs=[SMEM] + [VMEM] * 7,
        out_specs=VMEM,
        out_shape=shape_of((2, ROWS), F32),
        compiler_params=params(8),
        cost_estimate=cost(5.2),
        name="scores",
    )(flags, *found, rows, left, right)


def join_first_kernel(part_ref, out_ref):
    out_ref[...] = part_ref[...]


def join_second_kernel(part_ref, held_ref, out_ref):
    out_ref[...] = part_ref[...]


JOIN = 1024


def join_first(left):
    return pl.pallas_call(
        join_first_kernel,
        grid=(N_BLK * CAPP // JOIN,),
        in_specs=[pl.BlockSpec((JOIN, HALF), lambda i: (i, 0))],
        out_specs=pl.BlockSpec((JOIN, HALF), lambda i: (i, 0)),
        out_shape=shape_of((N_BLK * CAPP, D), BF16),
        compiler_params=params(10),
        cost_estimate=cost(8.0),
        name="join_first",
    )(left)


def join_second(right, held):
    return pl.pallas_call(
        join_second_kernel,
        grid=(N_BLK * CAPP // JOIN,),
        in_specs=[pl.BlockSpec((JOIN, HALF), lambda i: (i, 0)), ANY],
        out_specs=pl.BlockSpec((JOIN, HALF), lambda i: (i, 1)),
        out_shape=shape_of((N_BLK * CAPP, D), BF16),
        input_output_aliases={1: 0},
        compiler_params=params(10),
        cost_estimate=cost(5.2),
        name="join_second",
    )(right, held)


def along_y(value, k):
    return lax.ppermute(value, "blk", [(i, (i // 4 + k) % 4 * 4 + i % 4) for i in range(N_BLK)])


def along_z(value, k):
    return lax.ppermute(value, "cube", [(i, (i // 2 + k) % 4 * 2 + i % 2) for i in range(N_CUBE)])


def along_x(value, k):
    pairs = []
    for i in range(N_CUBE * N_BLK):
        cube, blk = i // N_BLK, i % N_BLK
        x = (blk // 2 % 2 * 2 + cube % 2 + k) % 4
        pairs.append((i, (cube // 2 * 2 + x % 2) * N_BLK + blk // 4 * 4 + x // 2 * 2 + blk % 2))
    return lax.ppermute(value, ("cube", "blk"), pairs)


def across(value, axis, bit):
    return lax.ppermute(value, axis, [(i, i ^ bit) for i in range(lax.axis_size(axis))])


def device(z, x_lo, y, x_hi, core):
    return (z * 2 + x_lo) * N_BLK + y * 4 + x_hi * 2 + core


PLACES = [(z, x_lo, y, x_hi, c) for z in range(4) for x_lo in (0, 1) for y in range(4) for x_hi in (0, 1) for c in (0, 1)]


def to_worker(value, k):
    pairs = [(device((p[0] + k) % 4, *p[1:]), device(*p)) for p in PLACES if p[0] % 2 == p[4]]
    return lax.ppermute(value, ("cube", "blk"), pairs)


def from_worker(value, dz, dc):
    pairs = [(device(*p), device(p[0] ^ dz, *p[1:4], p[4] ^ dc)) for p in PLACES if p[0] % 2 == p[4]]
    return lax.ppermute(value, ("cube", "blk"), pairs)


def after(value, earlier):
    return lax.optimization_barrier((value, earlier))[0]


def per_device(rows, start_vec, leave, owner):
    cube, blk = lax.axis_index("cube"), lax.axis_index("blk")
    z, x_lo = cube // 2, cube % 2
    y, core = blk // 4, blk % 2

    packed_l = pack_first(leave, rows, 0)
    arrived_l = across(packed_l, "cube", 1)
    leave_b = after(leave, packed_l)
    packed_r = pack_first(leave_b, rows, 1)
    row = slots(leave_b, owner.reshape(1, ROWS))

    flip = jnp.bitwise_xor(x_lo, core).astype(jnp.int32).reshape(1)
    leave_c, packed_r, row = lax.optimization_barrier((leave, packed_r, row))
    keep, send = gram(flip, leave_c, rows)
    got = across(send, "blk", 1)

    packed_r, arrived_l, keep = lax.optimization_barrier((packed_r, arrived_l, keep))
    arrived_r = across(packed_r, "cube", 1)
    next_l, packed_l = swap(row, rows, arrived_l, 0)
    arrived2_l = across(packed_l, "cube", 2)

    got = after(got, packed_l)

    def part(k):
        at = (y + k) % 4
        return lax.dynamic_index_in_dim(keep, at, 0, False) + lax.dynamic_index_in_dim(got, at, 0, False)

    parts = lax.optimization_barrier([part(k) for k in range(4)])
    moved = [along_y(parts[k], k) for k in (1, 2, 3)]

    next_r, packed_r = swap(row, rows, after(arrived_r, parts), 1)
    arrived2_r = across(packed_r, "cube", 2)
    leaf_l = leaf_pack(row, next_l, after(arrived2_l, packed_r))

    moved, _, arrived2_r = lax.optimization_barrier((moved, leaf_l, arrived2_r))
    out_l = lax.all_to_all(leaf_l, "blk", split_axis=0, concat_axis=0, tiled=True)
    own = parts[0] + moved[0] + moved[1] + moved[2]
    quarters = own.reshape(4, PIECE, LANES)
    parts = lax.optimization_barrier(
        [lax.dynamic_index_in_dim(quarters, (z + k) % 4, 0, False) for k in range(4)]
    )
    moved = [along_z(parts[k], k) for k in (1, 2, 3)]

    leaf_r = leaf_pack(row, next_r, after(arrived2_r, parts))

    moved = after(moved, leaf_r)
    own = parts[0] + moved[0] + moved[1] + moved[2]
    other = across(own, "blk", 1)
    both = own + other
    mine = jnp.where(core == 0, both, jnp.where(x_lo == 0, own, other))
    theirs = jnp.where(core == 0, both, jnp.where(x_lo == 0, other, own))
    piece = mine + along_x(mine, 2) + along_x(theirs, 1) + along_x(theirs, 3)
    near = [along_y(piece, -k) for k in (2, 1, 3)]
    leaf_r, _, out_l = lax.optimization_barrier((leaf_r, piece, out_l))
    out_r = lax.all_to_all(leaf_r, "blk", split_axis=0, concat_axis=0, tiled=True)
    held = join_first(after(out_l, leaf_r))
    held, near = lax.optimization_barrier((held, near))
    stack = jnp.stack([piece, near[1], near[0], near[2]])
    gathered = [stack] + [to_worker(stack, k) for k in (1, 2, 3)]

    place = jnp.stack([y, z]).astype(jnp.int32)
    members = jnp.where(core == 0, ROWS * N_BLK * N_CUBE, ROWS * N_BLK * N_CUBE // 2).astype(F32).reshape(1)
    found = power(place, members, start_vec.reshape(1, D), gathered)
    found = [found] + [from_worker(found, dz, dc) for dz, dc in ((0, 1), (1, 0), (1, 1))]
    flags = jnp.stack([core, z % 2]).astype(jnp.int32)
    scores = all_scores(flags, found, rows, next_l, next_r)
    return scores, join_second(out_r, held)


def solution(mesh):
    placed_at = (P(("cube", "blk"), None), P(), P(None, ("cube", "blk")), P(("cube", "blk"), None))
    return jax.shard_map(
        per_device,
        mesh=mesh,
        in_specs=placed_at,
        out_specs=(P(None, ("cube", "blk")), P(("cube", "blk"), None)),
        check_vma=False,
    )
```

```python
import jax
import jax.numpy as jnp
from jax import lax
from jax.experimental import pallas as pl
from jax.experimental.pallas import tpu as pltpu
from jax.sharding import PartitionSpec as P

D = 1024
ROWS = 1536
CAP = 768
CAPP = 192
N_BLK = 16
N_CUBE = 8
ITERS = 8
HALF = 512
LANES = 128
BLOCKS = [(i, j) for i in range(8) for j in range(i, 8)]
CHUNK = 9 * LANES
PIECE = CHUNK // 4
F32 = jnp.float32
BF16 = jnp.bfloat16


def params(mebibytes):
    return pltpu.CompilerParams(vmem_limit_bytes=mebibytes * 2**20)


def cost(microseconds):
    return pl.CostEstimate(
        flops=int(microseconds * 1.15e9), bytes_accessed=int(microseconds * 3.69e6), transcendentals=0
    )


VMEM = pl.BlockSpec(memory_space=pltpu.VMEM)
SMEM = pl.BlockSpec(memory_space=pltpu.SMEM)
ANY = pl.BlockSpec(memory_space=pl.ANY)


def iota(shape, dim):
    return lax.broadcasted_iota(jnp.int32, shape, dim)


def shape_of(shape, dtype):
    return jax.ShapeDtypeStruct(shape, dtype)


def running_count(flags):
    upper = jnp.where(iota((LANES, LANES), 0) <= iota((LANES, LANES), 1), 1.0, 0.0).astype(BF16)
    parts = []
    before = jnp.zeros((flags.shape[0], 1), F32)
    for b in range(ROWS // LANES):
        part = flags[:, b * LANES : (b + 1) * LANES].astype(BF16)
        part = jnp.dot(part, upper, preferred_element_type=F32) + before
        before = part[:, LANES - 1 : LANES]
        parts.append(part)
    return jnp.concatenate(parts, axis=1)


def slot_row(leave_ref, level):
    flags = jnp.broadcast_to(leave_ref[level : level + 1, :].astype(F32), (8, ROWS))
    return jnp.where(flags > 0.5, running_count(flags) - 1.0, -1.0)


def store_column(row, col_ref):
    for b in range(ROWS // LANES):
        part = jnp.broadcast_to(row[0:1, b * LANES : (b + 1) * LANES], (LANES, LANES))
        col_ref[b * LANES : (b + 1) * LANES, :] = part.T


def picker(row, first, count):
    slots = (iota((count, ROWS), 0) + first).astype(F32)
    return jnp.where(slots == row[0:1, :], 1.0, 0.0).astype(BF16)


def spreader(col, slots):
    parts = []
    for t in range(slots // LANES):
        lanes = (iota(col.shape, 1) + t * LANES).astype(F32)
        parts.append(jnp.where(col == lanes, 1.0, 0.0).astype(BF16))
    return jnp.concatenate(parts, axis=1)


def pack_first_kernel(leave_ref, rows_ref, out_ref):
    row = slot_row(leave_ref, 0)
    for t in range(CAP // 256):
        hot = picker(row, t * 256, 256)
        out_ref[t * 256 : (t + 1) * 256, :] = jnp.dot(hot, rows_ref[...], preferred_element_type=F32).astype(BF16)


def pack_first(leave, rows, half):
    return pl.pallas_call(
        pack_first_kernel,
        grid=(1,),
        in_specs=[pl.BlockSpec((2, ROWS), lambda i: (0, 0)), pl.BlockSpec((ROWS, HALF), lambda i: (0, half))],
        out_specs=pl.BlockSpec((CAP, HALF), lambda i: (0, 0)),
        out_shape=shape_of((CAP, HALF), BF16),
        compiler_params=params(8),
        cost_estimate=cost(4.3),
        name="pack_first",
    )(leave, in_hbm(rows))


def slots_kernel(leave_ref, owner_ref, row_ref):
    for level in range(2):
        row_ref[level * 8 : (level + 1) * 8, :] = slot_row(leave_ref, level)
    owner = jnp.broadcast_to(owner_ref[...], (N_BLK, ROWS))
    named = jnp.where(owner == iota((N_BLK, ROWS), 0), 1.0, 0.0)
    place = named * (running_count(named) - 1.0 + (iota((N_BLK, ROWS), 0) * CAPP).astype(F32))
    row_ref[16:24, :] = jnp.broadcast_to(jnp.sum(place, axis=0, keepdims=True), (8, ROWS))


def slots(leave, owner):
    return pl.pallas_call(
        slots_kernel,
        in_specs=[VMEM, VMEM],
        out_specs=VMEM,
        out_shape=shape_of((24, ROWS), F32),
        compiler_params=params(6),
        cost_estimate=cost(3.2),
        name="slots",
    )(leave, owner)


def in_hbm(value):
    return pltpu.with_memory_space_constraint(value, pltpu.HBM)


def placed(col, arrived, stay):
    moved = jnp.dot(spreader(col, CAP), arrived, preferred_element_type=F32).astype(BF16)
    leaves = jnp.concatenate([col] * (HALF // LANES), axis=1) >= 0.0
    return jnp.where(leaves, moved.astype(F32), stay.astype(F32)).astype(BF16)


def whole(shape):
    return pl.BlockSpec(shape, lambda i: (0,) * len(shape))


def swap_kernel(row_ref, rows_ref, arrived_ref, next_ref, packed_ref, col_ref):
    store_column(row_ref[0:8, :], col_ref)
    arrived = arrived_ref[...]
    for t in range(ROWS // 256):
        here = slice(t * 256, (t + 1) * 256)
        next_ref[here, :] = placed(col_ref[here, :], arrived, rows_ref[here, :])
    row = row_ref[8:16, :]
    for t in range(CAP // 256):
        hot = picker(row, t * 256, 256)
        packed_ref[t * 256 : (t + 1) * 256, :] = jnp.dot(hot, next_ref[...], preferred_element_type=F32).astype(BF16)


def swap(row, rows, arrived, half):
    return pl.pallas_call(
        swap_kernel,
        grid=(1,),
        in_specs=[whole((24, ROWS)), pl.BlockSpec((ROWS, HALF), lambda i: (0, half)), whole((CAP, HALF))],
        out_specs=[whole((ROWS, HALF)), whole((CAP, HALF))],
        out_shape=[shape_of((ROWS, HALF), BF16), shape_of((CAP, HALF), BF16)],
        scratch_shapes=[pltpu.VMEM((ROWS, LANES), F32)],
        compiler_params=params(12),
        cost_estimate=cost(20.0 if half == 0 else 5.3),
        name="swap",
    )(row, in_hbm(rows), arrived)


SLOTS = 768


def leaf_kernel(row_ref, rows_ref, arrived_ref, out_ref, last_ref, col_ref):
    @pl.when(pl.program_id(0) == 0)
    def _():
        store_column(row_ref[8:16, :], col_ref)
        arrived = arrived_ref[...]
        for t in range(ROWS // 256):
            here = slice(t * 256, (t + 1) * 256)
            last_ref[here, :] = placed(col_ref[here, :], arrived, rows_ref[here, :])

    row = row_ref[16:24, :] - (pl.program_id(0) * SLOTS).astype(F32)
    for t in range(SLOTS // 256):
        hot = picker(row, t * 256, 256)
        out_ref[t * 256 : (t + 1) * 256, :] = jnp.dot(hot, last_ref[...], preferred_element_type=F32).astype(BF16)


def leaf_pack(row, rows, arrived):
    return pl.pallas_call(
        leaf_kernel,
        grid=(N_BLK * CAPP // SLOTS,),
        in_specs=[whole((24, ROWS)), whole((ROWS, HALF)), whole((CAP, HALF))],
        out_specs=pl.BlockSpec((SLOTS, HALF), lambda i: (i, 0)),
        out_shape=pltpu.HBM((N_BLK * CAPP, HALF), BF16),
        scratch_shapes=[pltpu.VMEM((ROWS, HALF), BF16), pltpu.VMEM((ROWS, LANES), F32)],
        compiler_params=params(16),
        cost_estimate=cost(9.8),
        name="leaf_pack",
    )(row, rows, arrived)


def gram_kernel(flip_ref, leave_ref, rows_ref, keep_ref, send_ref, turned_ref, masked_ref):
    turned_ref[...] = rows_ref[...].T
    flag = jnp.bitwise_xor(jnp.broadcast_to(leave_ref[0:1, :], (8, ROWS)), flip_ref[0]).astype(F32)
    lane = iota((8, LANES), 1)
    sub = iota((8, LANES), 0)
    for out_ref, weight in ((keep_ref, flag), (send_ref, 1.0 - flag)):
        masked_ref[...] = turned_ref[...] * weight[0:1, :].astype(BF16)
        sums = jnp.dot(weight.astype(BF16), rows_ref[...], preferred_element_type=F32)
        for r in range(4):
            strip = jnp.dot(
                masked_ref[r * 256 : (r + 1) * 256, :], rows_ref[:, r * 256 :], preferred_element_type=F32
            )
            for i in (2 * r, 2 * r + 1):
                for j in range(i, 8):
                    at = BLOCKS.index((i, j))
                    top = (at % 9) * LANES
                    out_ref[at // 9, top : top + LANES, :] = strip[
                        (i - 2 * r) * LANES : (i - 2 * r + 1) * LANES, (j - 2 * r) * LANES : (j - 2 * r + 1) * LANES
                    ]
        for i in range(8):
            at = BLOCKS.index((i, i))
            top = (at % 9) * LANES + 120
            own = sums[:, i * LANES : (i + 1) * LANES]
            held = jnp.where((sub == 7) & (lane < 64), own, out_ref[at // 9, top : top + 8, :])
            out_ref[at // 9, top : top + 8, :] = jnp.where((sub == 6) & (lane < 64), pltpu.roll(own, 64, 1), held)


def gram(flip, leave, rows):
    return pl.pallas_call(
        gram_kernel,
        in_specs=[SMEM, VMEM, VMEM],
        out_specs=[VMEM, VMEM],
        out_shape=[shape_of((4, CHUNK, LANES), F32)] * 2,
        scratch_shapes=[pltpu.VMEM((D, ROWS), BF16)] * 2,
        compiler_params=params(22),
        cost_estimate=cost(8.6),
        name="gram",
    )(flip, leave, rows)


def power_kernel(place_ref, members_ref, start_ref, a_ref, b_ref, c_ref, d_ref, out_ref, packed_ref, mat_ref):
    y, z = place_ref[0], place_ref[1]
    for k, part_ref in enumerate((a_ref, b_ref, c_ref, d_ref)):
        for m in range(4):
            at = (lax.rem(y + m, 4) * 4 + lax.rem(z + k, 4)) * PIECE
            packed_ref[pl.ds(pl.multiple_of(at, 8), PIECE), :] = part_ref[m]
    members = members_ref[0]
    lane = iota((8, LANES), 1)
    wide_lane, wide_sub = iota((LANES, LANES), 1), iota((LANES, LANES), 0)
    sums_row, sums_col = [], []
    for i in range(8):
        top = BLOCKS.index((i, i)) * LANES
        tail = packed_ref[top + 120 : top + 128, :]
        row = jnp.where(lane[0:1] < 64, tail[7:8, :], pltpu.roll(tail, 64, 1)[6:7, :])
        sums_row.append(row)
        sums_col.append(jnp.broadcast_to(row, (LANES, LANES)).T)
    for i in range(8):
        for j in range(i, 8):
            top = BLOCKS.index((i, j)) * LANES
            block = packed_ref[top : top + LANES, :]
            other = block.T
            if i == j:
                block = jnp.where((wide_sub >= 126) & (wide_lane < 64), other, block)
            hi, hj = slice(i * LANES, (i + 1) * LANES), slice(j * LANES, (j + 1) * LANES)
            mat_ref[hi, hj] = block - sums_col[i] * (sums_row[j] / members)
            if i != j:
                mat_ref[hj, hi] = other - sums_col[j] * (sums_row[i] / members)
    start = start_ref[...]
    vec = start / jnp.sqrt(jnp.sum(start * start, axis=1, keepdims=True))
    for _ in range(ITERS // 2):
        cols = []
        square = jnp.zeros((8, 1), F32)
        for i in range(8):
            total = jnp.zeros((LANES, LANES), F32)
            for j in range(8):
                total = total + mat_ref[i * LANES : (i + 1) * LANES, j * LANES : (j + 1) * LANES] * vec[
                    :, j * LANES : (j + 1) * LANES
                ]
            col = jnp.sum(total, axis=1, keepdims=True)
            cols.append(col)
        norm = sum(jnp.sum(col * col, axis=0, keepdims=True) for col in cols)
        norm = jnp.sqrt(norm)
        total = jnp.zeros((8, D), F32)
        for i in range(8):
            col = cols[i] / norm
            for s in range(LANES // 8):
                at = i * LANES + s * 8
                total = total + mat_ref[at : at + 8, :] * col[s * 8 : (s + 1) * 8, :]
        vec = jnp.sum(total, axis=0, keepdims=True)
        vec = vec / jnp.sqrt(jnp.sum(vec * vec, axis=1, keepdims=True))
    sums = jnp.concatenate(sums_row, axis=1)
    offset = jnp.sum(sums * vec, axis=1, keepdims=True) / members
    out_ref[0:8, :] = jnp.where(iota((8, D), 0) == 0, vec, offset)


def power(place, members, start, parts):
    return pl.pallas_call(
        power_kernel,
        in_specs=[SMEM, SMEM, VMEM] + [VMEM] * 4,
        out_specs=VMEM,
        out_shape=shape_of((8, D), F32),
        scratch_shapes=[pltpu.VMEM((len(BLOCKS) * LANES, LANES), F32), pltpu.VMEM((D, D), F32)],
        compiler_params=params(12),
        cost_estimate=cost(6.6),
        name="power",
    )(place, members, start, *parts)


def project(vec, blocks):
    sub = None
    total = None
    at = 0
    for block in blocks:
        here = vec[:, at : at + block.shape[1]]
        at += block.shape[1]
        high = here.astype(BF16)
        rest = here - high.astype(F32)
        mid = rest.astype(BF16)
        low = (rest - mid.astype(F32)).astype(BF16)
        sub = iota((8, here.shape[1]), 0)
        terms = jnp.where(
            sub == 0,
            high.astype(F32),
            jnp.where(sub == 1, mid.astype(F32), jnp.where(sub == 2, low.astype(F32), 0.0)),
        ).astype(BF16)
        part = lax.dot_general(terms, block, (((1,), (1,)), ((), ())), preferred_element_type=F32)
        total = part if total is None else total + part
    return total[0:1, :] + total[1:2, :] + total[2:3, :]


def scores_kernel(flags_ref, own_ref, core_ref, z_ref, both_ref, rows_ref, left_ref, right_ref, out_ref):
    worker = flags_ref[0] == flags_ref[1]
    same = jnp.where(worker, own_ref[...], core_ref[...])
    unlike = jnp.where(worker, both_ref[...], z_ref[...])
    even = flags_ref[1] == 0
    top = jnp.where(even, same, unlike)
    low = jnp.where(even, unlike, same)
    out_ref[0:1, :] = project(top[0:1, :], [rows_ref[...]]) - top[1:2, 0:1]
    out_ref[1:2, :] = project(low[0:1, :], [left_ref[...], right_ref[...]]) - low[1:2, 0:1]


def all_scores(flags, found, rows, left, right):
    return pl.pallas_call(
        scores_kernel,
        in_specs=[SMEM] + [VMEM] * 7,
        out_specs=VMEM,
        out_shape=shape_of((2, ROWS), F32),
        compiler_params=params(8),
        cost_estimate=cost(5.2),
        name="scores",
    )(flags, *found, rows, left, right)


def join_first_kernel(part_ref, out_ref):
    out_ref[...] = part_ref[...]


def join_second_kernel(part_ref, held_ref, out_ref, buffer_ref, in_sem, out_sem):
    copies = []
    for i in range(PIECES):
        here = pl.ds(i * (N_BLK * CAPP // PIECES), N_BLK * CAPP // PIECES)
        copies.append(
            (
                pltpu.make_async_copy(part_ref.at[here], buffer_ref.at[here], in_sem.at[i]),
                pltpu.make_async_copy(buffer_ref.at[here], out_ref.at[here, pl.ds(HALF, HALF)], out_sem.at[i]),
            )
        )
    for arriving, _ in copies:
        arriving.start()
    for arriving, leaving in copies:
        arriving.wait()
        leaving.start()
    for _, leaving in copies:
        leaving.wait()


JOIN = 1024
PIECES = 8


def join_first(left):
    return pl.pallas_call(
        join_first_kernel,
        grid=(N_BLK * CAPP // JOIN,),
        in_specs=[pl.BlockSpec((JOIN, HALF), lambda i: (i, 0))],
        out_specs=pl.BlockSpec((JOIN, HALF), lambda i: (i, 0)),
        out_shape=shape_of((N_BLK * CAPP, D), BF16),
        compiler_params=params(10),
        cost_estimate=cost(8.0),
        name="join_first",
    )(left)


def join_second(right, held):
    return pl.pallas_call(
        join_second_kernel,
        in_specs=[ANY, ANY],
        out_specs=ANY,
        out_shape=shape_of((N_BLK * CAPP, D), BF16),
        scratch_shapes=[
            pltpu.VMEM((N_BLK * CAPP, HALF), BF16),
            pltpu.SemaphoreType.DMA((PIECES,)),
            pltpu.SemaphoreType.DMA((PIECES,)),
        ],
        input_output_aliases={1: 0},
        compiler_params=params(10),
        cost_estimate=cost(5.2),
        name="join_second",
    )(right, held)


def along_y(value, k):
    return lax.ppermute(value, "blk", [(i, (i // 4 + k) % 4 * 4 + i % 4) for i in range(N_BLK)])


def along_z(value, k):
    return lax.ppermute(value, "cube", [(i, (i // 2 + k) % 4 * 2 + i % 2) for i in range(N_CUBE)])


def along_x(value, k):
    pairs = []
    for i in range(N_CUBE * N_BLK):
        cube, blk = i // N_BLK, i % N_BLK
        x = (blk // 2 % 2 * 2 + cube % 2 + k) % 4
        pairs.append((i, (cube // 2 * 2 + x % 2) * N_BLK + blk // 4 * 4 + x // 2 * 2 + blk % 2))
    return lax.ppermute(value, ("cube", "blk"), pairs)


def across(value, axis, bit):
    return lax.ppermute(value, axis, [(i, i ^ bit) for i in range(lax.axis_size(axis))])


def device(z, x_lo, y, x_hi, core):
    return (z * 2 + x_lo) * N_BLK + y * 4 + x_hi * 2 + core


PLACES = [(z, x_lo, y, x_hi, c) for z in range(4) for x_lo in (0, 1) for y in range(4) for x_hi in (0, 1) for c in (0, 1)]


def to_worker(value, k):
    pairs = [(device((p[0] + k) % 4, *p[1:]), device(*p)) for p in PLACES if p[0] % 2 == p[4]]
    return lax.ppermute(value, ("cube", "blk"), pairs)


def from_worker(value, dz, dc):
    pairs = [(device(*p), device(p[0] ^ dz, *p[1:4], p[4] ^ dc)) for p in PLACES if p[0] % 2 == p[4]]
    return lax.ppermute(value, ("cube", "blk"), pairs)


def after(value, earlier):
    return lax.optimization_barrier((value, earlier))[0]


def per_device(rows, start_vec, leave, owner):
    cube, blk = lax.axis_index("cube"), lax.axis_index("blk")
    z, x_lo = cube // 2, cube % 2
    y, core = blk // 4, blk % 2

    packed_l = pack_first(leave, rows, 0)
    arrived_l = across(packed_l, "cube", 1)
    leave_b = after(leave, packed_l)
    packed_r = pack_first(leave_b, rows, 1)
    row = slots(leave_b, owner.reshape(1, ROWS))

    flip = jnp.bitwise_xor(x_lo, core).astype(jnp.int32).reshape(1)
    leave_c, packed_r, row = lax.optimization_barrier((leave, packed_r, row))
    keep, send = gram(flip, leave_c, rows)
    got = across(send, "blk", 1)

    packed_r, arrived_l, keep = lax.optimization_barrier((packed_r, arrived_l, keep))
    arrived_r = across(packed_r, "cube", 1)
    next_l, packed_l = swap(row, rows, arrived_l, 0)
    arrived2_l = across(packed_l, "cube", 2)

    got = after(got, packed_l)

    def part(k):
        at = (y + k) % 4
        return lax.dynamic_index_in_dim(keep, at, 0, False) + lax.dynamic_index_in_dim(got, at, 0, False)

    parts = lax.optimization_barrier([part(k) for k in range(4)])
    moved = [along_y(parts[k], k) for k in (1, 2, 3)]

    next_r, packed_r = swap(row, rows, after(arrived_r, parts), 1)
    arrived2_r = across(packed_r, "cube", 2)
    leaf_l = leaf_pack(row, next_l, after(arrived2_l, packed_r))

    moved, _, arrived2_r = lax.optimization_barrier((moved, leaf_l, arrived2_r))
    out_l = lax.all_to_all(leaf_l, "blk", split_axis=0, concat_axis=0, tiled=True)
    own = parts[0] + moved[0] + moved[1] + moved[2]
    quarters = own.reshape(4, PIECE, LANES)
    parts = lax.optimization_barrier(
        [lax.dynamic_index_in_dim(quarters, (z + k) % 4, 0, False) for k in range(4)]
    )
    moved = [along_z(parts[k], k) for k in (1, 2, 3)]

    leaf_r = leaf_pack(row, next_r, after(arrived2_r, parts))

    moved = after(moved, leaf_r)
    own = parts[0] + moved[0] + moved[1] + moved[2]
    other = across(own, "blk", 1)
    both = own + other
    mine = jnp.where(core == 0, both, jnp.where(x_lo == 0, own, other))
    theirs = jnp.where(core == 0, both, jnp.where(x_lo == 0, other, own))
    piece = mine + along_x(mine, 2) + along_x(theirs, 1) + along_x(theirs, 3)
    near = [along_y(piece, -k) for k in (2, 1, 3)]
    leaf_r, _, out_l = lax.optimization_barrier((leaf_r, piece, out_l))
    out_r = lax.all_to_all(leaf_r, "blk", split_axis=0, concat_axis=0, tiled=True)
    held = join_first(after(out_l, leaf_r))
    held, near = lax.optimization_barrier((held, near))
    stack = jnp.stack([piece, near[1], near[0], near[2]])
    gathered = [stack] + [to_worker(stack, k) for k in (1, 2, 3)]

    place = jnp.stack([y, z]).astype(jnp.int32)
    members = jnp.where(core == 0, ROWS * N_BLK * N_CUBE, ROWS * N_BLK * N_CUBE // 2).astype(F32).reshape(1)
    found = power(place, members, start_vec.reshape(1, D), gathered)
    found = [found] + [from_worker(found, dz, dc) for dz, dc in ((0, 1), (1, 0), (1, 1))]
    flags = jnp.stack([core, z % 2]).astype(jnp.int32)
    scores = all_scores(flags, found, rows, next_l, next_r)
    return scores, join_second(out_r, held)


def solution(mesh):
    placed_at = (P(("cube", "blk"), None), P(), P(None, ("cube", "blk")), P(("cube", "blk"), None))
    return jax.shard_map(
        per_device,
        mesh=mesh,
        in_specs=placed_at,
        out_specs=(P(None, ("cube", "blk")), P(("cube", "blk"), None)),
        check_vma=False,
    )
```

```python
import jax
import jax.numpy as jnp
from jax import lax
from jax.experimental import pallas as pl
from jax.experimental.pallas import tpu as pltpu
from jax.sharding import PartitionSpec as P

D = 1024
ROWS = 1536
CAP = 768
CAPP = 192
N_BLK = 16
N_CUBE = 8
ITERS = 8
HALF = 512
LANES = 128
BLOCKS = [(i, j) for i in range(8) for j in range(i, 8)]
CHUNK = 9 * LANES
PIECE = CHUNK // 4
F32 = jnp.float32
BF16 = jnp.bfloat16


def params(mebibytes):
    return pltpu.CompilerParams(vmem_limit_bytes=mebibytes * 2**20)


def cost(microseconds):
    return pl.CostEstimate(
        flops=int(microseconds * 1.15e9), bytes_accessed=int(microseconds * 3.69e6), transcendentals=0
    )


VMEM = pl.BlockSpec(memory_space=pltpu.VMEM)
SMEM = pl.BlockSpec(memory_space=pltpu.SMEM)
ANY = pl.BlockSpec(memory_space=pl.ANY)


def iota(shape, dim):
    return lax.broadcasted_iota(jnp.int32, shape, dim)


def shape_of(shape, dtype):
    return jax.ShapeDtypeStruct(shape, dtype)


def running_count(flags):
    upper = jnp.where(iota((LANES, LANES), 0) <= iota((LANES, LANES), 1), 1.0, 0.0).astype(BF16)
    parts = []
    before = jnp.zeros((flags.shape[0], 1), F32)
    for b in range(ROWS // LANES):
        part = flags[:, b * LANES : (b + 1) * LANES].astype(BF16)
        part = jnp.dot(part, upper, preferred_element_type=F32) + before
        before = part[:, LANES - 1 : LANES]
        parts.append(part)
    return jnp.concatenate(parts, axis=1)


def slot_row(leave_ref, level):
    flags = jnp.broadcast_to(leave_ref[level : level + 1, :].astype(F32), (8, ROWS))
    return jnp.where(flags > 0.5, running_count(flags) - 1.0, -1.0)


def store_column(row, col_ref):
    for b in range(ROWS // LANES):
        part = jnp.broadcast_to(row[0:1, b * LANES : (b + 1) * LANES], (LANES, LANES))
        col_ref[b * LANES : (b + 1) * LANES, :] = part.T


def picker(row, first, count):
    slots = (iota((count, ROWS), 0) + first).astype(F32)
    return jnp.where(slots == row[0:1, :], 1.0, 0.0).astype(BF16)


def spreader(col, slots):
    parts = []
    for t in range(slots // LANES):
        lanes = (iota(col.shape, 1) + t * LANES).astype(F32)
        parts.append(jnp.where(col == lanes, 1.0, 0.0).astype(BF16))
    return jnp.concatenate(parts, axis=1)


def pack_first_kernel(leave_ref, rows_ref, out_ref):
    row = slot_row(leave_ref, 0)
    for t in range(CAP // 256):
        hot = picker(row, t * 256, 256)
        out_ref[t * 256 : (t + 1) * 256, :] = jnp.dot(hot, rows_ref[...], preferred_element_type=F32).astype(BF16)


def pack_first(leave, rows, half):
    return pl.pallas_call(
        pack_first_kernel,
        grid=(1,),
        in_specs=[pl.BlockSpec((2, ROWS), lambda i: (0, 0)), pl.BlockSpec((ROWS, HALF), lambda i: (0, half))],
        out_specs=pl.BlockSpec((CAP, HALF), lambda i: (0, 0)),
        out_shape=shape_of((CAP, HALF), BF16),
        compiler_params=params(8),
        cost_estimate=cost(4.3),
        name="pack_first",
    )(leave, in_hbm(rows))


def slots_kernel(leave_ref, owner_ref, row_ref):
    for level in range(2):
        row_ref[level * 8 : (level + 1) * 8, :] = slot_row(leave_ref, level)
    owner = jnp.broadcast_to(owner_ref[...], (N_BLK, ROWS))
    named = jnp.where(owner == iota((N_BLK, ROWS), 0), 1.0, 0.0)
    place = named * (running_count(named) - 1.0 + (iota((N_BLK, ROWS), 0) * CAPP).astype(F32))
    row_ref[16:24, :] = jnp.broadcast_to(jnp.sum(place, axis=0, keepdims=True), (8, ROWS))


def slots(leave, owner):
    return pl.pallas_call(
        slots_kernel,
        in_specs=[VMEM, VMEM],
        out_specs=VMEM,
        out_shape=shape_of((24, ROWS), F32),
        compiler_params=params(6),
        cost_estimate=cost(3.2),
        name="slots",
    )(leave, owner)


def in_hbm(value):
    return pltpu.with_memory_space_constraint(value, pltpu.HBM)


def placed(col, arrived, stay):
    moved = jnp.dot(spreader(col, CAP), arrived, preferred_element_type=F32).astype(BF16)
    leaves = jnp.concatenate([col] * (HALF // LANES), axis=1) >= 0.0
    return jnp.where(leaves, moved.astype(F32), stay.astype(F32)).astype(BF16)


def whole(shape):
    return pl.BlockSpec(shape, lambda i: (0,) * len(shape))


def swap_kernel(row_ref, rows_ref, arrived_ref, next_ref, packed_ref, col_ref):
    store_column(row_ref[0:8, :], col_ref)
    arrived = arrived_ref[...]
    for t in range(ROWS // 256):
        here = slice(t * 256, (t + 1) * 256)
        next_ref[here, :] = placed(col_ref[here, :], arrived, rows_ref[here, :])
    row = row_ref[8:16, :]
    for t in range(CAP // 256):
        hot = picker(row, t * 256, 256)
        packed_ref[t * 256 : (t + 1) * 256, :] = jnp.dot(hot, next_ref[...], preferred_element_type=F32).astype(BF16)


def swap(row, rows, arrived, half):
    return pl.pallas_call(
        swap_kernel,
        grid=(1,),
        in_specs=[whole((24, ROWS)), pl.BlockSpec((ROWS, HALF), lambda i: (0, half)), whole((CAP, HALF))],
        out_specs=[whole((ROWS, HALF)), whole((CAP, HALF))],
        out_shape=[(shape_of if half == 0 else pltpu.HBM)((ROWS, HALF), BF16), shape_of((CAP, HALF), BF16)],
        scratch_shapes=[pltpu.VMEM((ROWS, LANES), F32)],
        compiler_params=params(12),
        cost_estimate=cost(20.0 if half == 0 else 5.3),
        name="swap",
    )(row, in_hbm(rows), arrived)


SLOTS = 768


def leaf_kernel(row_ref, rows_ref, arrived_ref, out_ref, last_ref, col_ref):
    @pl.when(pl.program_id(0) == 0)
    def _():
        store_column(row_ref[8:16, :], col_ref)
        arrived = arrived_ref[...]
        for t in range(ROWS // 256):
            here = slice(t * 256, (t + 1) * 256)
            last_ref[here, :] = placed(col_ref[here, :], arrived, rows_ref[here, :])

    row = row_ref[16:24, :] - (pl.program_id(0) * SLOTS).astype(F32)
    for t in range(SLOTS // 256):
        hot = picker(row, t * 256, 256)
        out_ref[t * 256 : (t + 1) * 256, :] = jnp.dot(hot, last_ref[...], preferred_element_type=F32).astype(BF16)


def leaf_pack(row, rows, arrived):
    return pl.pallas_call(
        leaf_kernel,
        grid=(N_BLK * CAPP // SLOTS,),
        in_specs=[whole((24, ROWS)), whole((ROWS, HALF)), whole((CAP, HALF))],
        out_specs=pl.BlockSpec((SLOTS, HALF), lambda i: (i, 0)),
        out_shape=pltpu.HBM((N_BLK * CAPP, HALF), BF16),
        scratch_shapes=[pltpu.VMEM((ROWS, HALF), BF16), pltpu.VMEM((ROWS, LANES), F32)],
        compiler_params=params(16),
        cost_estimate=cost(9.8),
        name="leaf_pack",
    )(row, rows, arrived)


def gram_kernel(flip_ref, leave_ref, rows_ref, keep_ref, send_ref, turned_ref, masked_ref):
    turned_ref[...] = rows_ref[...].T
    flag = jnp.bitwise_xor(jnp.broadcast_to(leave_ref[0:1, :], (8, ROWS)), flip_ref[0]).astype(F32)
    lane = iota((8, LANES), 1)
    sub = iota((8, LANES), 0)
    for out_ref, weight in ((keep_ref, flag), (send_ref, 1.0 - flag)):
        masked_ref[...] = turned_ref[...] * weight[0:1, :].astype(BF16)
        sums = jnp.dot(weight.astype(BF16), rows_ref[...], preferred_element_type=F32)
        for r in range(4):
            strip = jnp.dot(
                masked_ref[r * 256 : (r + 1) * 256, :], rows_ref[:, r * 256 :], preferred_element_type=F32
            )
            for i in (2 * r, 2 * r + 1):
                for j in range(i, 8):
                    at = BLOCKS.index((i, j))
                    top = (at % 9) * LANES
                    out_ref[at // 9, top : top + LANES, :] = strip[
                        (i - 2 * r) * LANES : (i - 2 * r + 1) * LANES, (j - 2 * r) * LANES : (j - 2 * r + 1) * LANES
                    ]
        for i in range(8):
            at = BLOCKS.index((i, i))
            top = (at % 9) * LANES + 120
            own = sums[:, i * LANES : (i + 1) * LANES]
            held = jnp.where((sub == 7) & (lane < 64), own, out_ref[at // 9, top : top + 8, :])
            out_ref[at // 9, top : top + 8, :] = jnp.where((sub == 6) & (lane < 64), pltpu.roll(own, 64, 1), held)


def gram(flip, leave, rows):
    return pl.pallas_call(
        gram_kernel,
        in_specs=[SMEM, VMEM, VMEM],
        out_specs=[VMEM, VMEM],
        out_shape=[shape_of((4, CHUNK, LANES), F32)] * 2,
        scratch_shapes=[pltpu.VMEM((D, ROWS), BF16)] * 2,
        compiler_params=params(22),
        cost_estimate=cost(8.6),
        name="gram",
    )(flip, leave, rows)


def power_kernel(place_ref, members_ref, start_ref, a_ref, b_ref, c_ref, d_ref, out_ref, packed_ref, mat_ref):
    y, z = place_ref[0], place_ref[1]
    for k, part_ref in enumerate((a_ref, b_ref, c_ref, d_ref)):
        for m in range(4):
            at = (lax.rem(y + m, 4) * 4 + lax.rem(z + k, 4)) * PIECE
            packed_ref[pl.ds(pl.multiple_of(at, 8), PIECE), :] = part_ref[m]
    members = members_ref[0]
    lane = iota((8, LANES), 1)
    wide_lane, wide_sub = iota((LANES, LANES), 1), iota((LANES, LANES), 0)
    sums_row, sums_col = [], []
    for i in range(8):
        top = BLOCKS.index((i, i)) * LANES
        tail = packed_ref[top + 120 : top + 128, :]
        row = jnp.where(lane[0:1] < 64, tail[7:8, :], pltpu.roll(tail, 64, 1)[6:7, :])
        sums_row.append(row)
        sums_col.append(jnp.broadcast_to(row, (LANES, LANES)).T)
    for i in range(8):
        for j in range(i, 8):
            top = BLOCKS.index((i, j)) * LANES
            block = packed_ref[top : top + LANES, :]
            other = block.T
            if i == j:
                block = jnp.where((wide_sub >= 126) & (wide_lane < 64), other, block)
            hi, hj = slice(i * LANES, (i + 1) * LANES), slice(j * LANES, (j + 1) * LANES)
            mat_ref[hi, hj] = block - sums_col[i] * (sums_row[j] / members)
            if i != j:
                mat_ref[hj, hi] = other - sums_col[j] * (sums_row[i] / members)
    start = start_ref[...]
    vec = start / jnp.sqrt(jnp.sum(start * start, axis=1, keepdims=True))
    for _ in range(ITERS // 2):
        cols = []
        square = jnp.zeros((8, 1), F32)
        for i in range(8):
            total = jnp.zeros((LANES, LANES), F32)
            for j in range(8):
                total = total + mat_ref[i * LANES : (i + 1) * LANES, j * LANES : (j + 1) * LANES] * vec[
                    :, j * LANES : (j + 1) * LANES
                ]
            col = jnp.sum(total, axis=1, keepdims=True)
            cols.append(col)
        norm = sum(jnp.sum(col * col, axis=0, keepdims=True) for col in cols)
        norm = jnp.sqrt(norm)
        total = jnp.zeros((8, D), F32)
        for i in range(8):
            col = cols[i] / norm
            for s in range(LANES // 8):
                at = i * LANES + s * 8
                total = total + mat_ref[at : at + 8, :] * col[s * 8 : (s + 1) * 8, :]
        vec = jnp.sum(total, axis=0, keepdims=True)
        vec = vec / jnp.sqrt(jnp.sum(vec * vec, axis=1, keepdims=True))
    sums = jnp.concatenate(sums_row, axis=1)
    offset = jnp.sum(sums * vec, axis=1, keepdims=True) / members
    out_ref[0:8, :] = jnp.where(iota((8, D), 0) == 0, vec, offset)


def power(place, members, start, parts):
    return pl.pallas_call(
        power_kernel,
        in_specs=[SMEM, SMEM, VMEM] + [VMEM] * 4,
        out_specs=VMEM,
        out_shape=shape_of((8, D), F32),
        scratch_shapes=[pltpu.VMEM((len(BLOCKS) * LANES, LANES), F32), pltpu.VMEM((D, D), F32)],
        compiler_params=params(12),
        cost_estimate=cost(6.6),
        name="power",
    )(place, members, start, *parts)


def project(vec, blocks):
    sub = None
    total = None
    at = 0
    for block in blocks:
        here = vec[:, at : at + block.shape[1]]
        at += block.shape[1]
        high = here.astype(BF16)
        rest = here - high.astype(F32)
        mid = rest.astype(BF16)
        low = (rest - mid.astype(F32)).astype(BF16)
        sub = iota((8, here.shape[1]), 0)
        terms = jnp.where(
            sub == 0,
            high.astype(F32),
            jnp.where(sub == 1, mid.astype(F32), jnp.where(sub == 2, low.astype(F32), 0.0)),
        ).astype(BF16)
        part = lax.dot_general(terms, block, (((1,), (1,)), ((), ())), preferred_element_type=F32)
        total = part if total is None else total + part
    return total[0:1, :] + total[1:2, :] + total[2:3, :]


def scores_kernel(flags_ref, own_ref, core_ref, z_ref, both_ref, rows_ref, left_ref, right_ref, out_ref):
    worker = flags_ref[0] == flags_ref[1]
    same = jnp.where(worker, own_ref[...], core_ref[...])
    unlike = jnp.where(worker, both_ref[...], z_ref[...])
    even = flags_ref[1] == 0
    top = jnp.where(even, same, unlike)
    low = jnp.where(even, unlike, same)
    out_ref[0:1, :] = project(top[0:1, :], [rows_ref[...]]) - top[1:2, 0:1]
    out_ref[1:2, :] = project(low[0:1, :], [left_ref[...], right_ref[...]]) - low[1:2, 0:1]


def all_scores(flags, found, rows, left, right):
    return pl.pallas_call(
        scores_kernel,
        in_specs=[SMEM] + [VMEM] * 7,
        out_specs=VMEM,
        out_shape=shape_of((2, ROWS), F32),
        compiler_params=params(8),
        cost_estimate=cost(5.2),
        name="scores",
    )(flags, *found, rows, left, right)


def join_first_kernel(part_ref, out_ref):
    out_ref[...] = part_ref[...]


def join_second_kernel(part_ref, held_ref, out_ref, buffer_ref, in_sem, out_sem):
    copies = []
    for i in range(PIECES):
        here = pl.ds(i * (N_BLK * CAPP // PIECES), N_BLK * CAPP // PIECES)
        copies.append(
            (
                pltpu.make_async_copy(part_ref.at[here], buffer_ref.at[here], in_sem.at[i]),
                pltpu.make_async_copy(buffer_ref.at[here], out_ref.at[here, pl.ds(HALF, HALF)], out_sem.at[i]),
            )
        )
    for arriving, _ in copies:
        arriving.start()
    for arriving, leaving in copies:
        arriving.wait()
        leaving.start()
    for _, leaving in copies:
        leaving.wait()


JOIN = 1024
PIECES = 8


def join_first(left):
    return pl.pallas_call(
        join_first_kernel,
        grid=(N_BLK * CAPP // JOIN,),
        in_specs=[pl.BlockSpec((JOIN, HALF), lambda i: (i, 0))],
        out_specs=pl.BlockSpec((JOIN, HALF), lambda i: (i, 0)),
        out_shape=shape_of((N_BLK * CAPP, D), BF16),
        compiler_params=params(10),
        cost_estimate=cost(8.0),
        name="join_first",
    )(left)


def join_second(right, held):
    return pl.pallas_call(
        join_second_kernel,
        in_specs=[ANY, ANY],
        out_specs=ANY,
        out_shape=shape_of((N_BLK * CAPP, D), BF16),
        scratch_shapes=[
            pltpu.VMEM((N_BLK * CAPP, HALF), BF16),
            pltpu.SemaphoreType.DMA((PIECES,)),
            pltpu.SemaphoreType.DMA((PIECES,)),
        ],
        input_output_aliases={1: 0},
        compiler_params=params(10),
        cost_estimate=cost(5.2),
        name="join_second",
    )(right, held)


def along_y(value, k):
    return lax.ppermute(value, "blk", [(i, (i // 4 + k) % 4 * 4 + i % 4) for i in range(N_BLK)])


def along_z(value, k):
    return lax.ppermute(value, "cube", [(i, (i // 2 + k) % 4 * 2 + i % 2) for i in range(N_CUBE)])


def along_x(value, k):
    pairs = []
    for i in range(N_CUBE * N_BLK):
        cube, blk = i // N_BLK, i % N_BLK
        x = (blk // 2 % 2 * 2 + cube % 2 + k) % 4
        pairs.append((i, (cube // 2 * 2 + x % 2) * N_BLK + blk // 4 * 4 + x // 2 * 2 + blk % 2))
    return lax.ppermute(value, ("cube", "blk"), pairs)


def across(value, axis, bit):
    return lax.ppermute(value, axis, [(i, i ^ bit) for i in range(lax.axis_size(axis))])


def device(z, x_lo, y, x_hi, core):
    return (z * 2 + x_lo) * N_BLK + y * 4 + x_hi * 2 + core


PLACES = [(z, x_lo, y, x_hi, c) for z in range(4) for x_lo in (0, 1) for y in range(4) for x_hi in (0, 1) for c in (0, 1)]


def to_worker(value, k):
    pairs = [(device((p[0] + k) % 4, *p[1:]), device(*p)) for p in PLACES if p[0] % 2 == p[4]]
    return lax.ppermute(value, ("cube", "blk"), pairs)


def from_worker(value, dz, dc):
    pairs = [(device(*p), device(p[0] ^ dz, *p[1:4], p[4] ^ dc)) for p in PLACES if p[0] % 2 == p[4]]
    return lax.ppermute(value, ("cube", "blk"), pairs)


def after(value, earlier):
    return lax.optimization_barrier((value, earlier))[0]


def per_device(rows, start_vec, leave, owner):
    cube, blk = lax.axis_index("cube"), lax.axis_index("blk")
    z, x_lo = cube // 2, cube % 2
    y, core = blk // 4, blk % 2

    packed_l = pack_first(leave, rows, 0)
    arrived_l = across(packed_l, "cube", 1)
    leave_b = after(leave, packed_l)
    packed_r = pack_first(leave_b, rows, 1)
    row = slots(leave_b, owner.reshape(1, ROWS))

    flip = jnp.bitwise_xor(x_lo, core).astype(jnp.int32).reshape(1)
    leave_c, packed_r, row = lax.optimization_barrier((leave, packed_r, row))
    keep, send = gram(flip, leave_c, rows)
    got = across(send, "blk", 1)

    packed_r, arrived_l, keep = lax.optimization_barrier((packed_r, arrived_l, keep))
    arrived_r = across(packed_r, "cube", 1)
    next_l, packed_l = swap(row, rows, arrived_l, 0)
    arrived2_l = across(packed_l, "cube", 2)

    got = after(got, packed_l)

    def part(k):
        at = (y + k) % 4
        return lax.dynamic_index_in_dim(keep, at, 0, False) + lax.dynamic_index_in_dim(got, at, 0, False)

    parts = lax.optimization_barrier([part(k) for k in range(4)])
    moved = [along_y(parts[k], k) for k in (1, 2, 3)]

    next_r, packed_r = swap(row, rows, after(arrived_r, parts), 1)
    arrived2_r = across(packed_r, "cube", 2)
    leaf_l = leaf_pack(row, next_l, after(arrived2_l, packed_r))

    moved, _, arrived2_r = lax.optimization_barrier((moved, leaf_l, arrived2_r))
    out_l = lax.all_to_all(leaf_l, "blk", split_axis=0, concat_axis=0, tiled=True)
    own = parts[0] + moved[0] + moved[1] + moved[2]
    quarters = own.reshape(4, PIECE, LANES)
    parts = lax.optimization_barrier(
        [lax.dynamic_index_in_dim(quarters, (z + k) % 4, 0, False) for k in range(4)]
    )
    moved = [along_z(parts[k], k) for k in (1, 2, 3)]

    leaf_r = leaf_pack(row, next_r, after(arrived2_r, parts))

    moved = after(moved, leaf_r)
    own = parts[0] + moved[0] + moved[1] + moved[2]
    other = across(own, "blk", 1)
    both = own + other
    mine = jnp.where(core == 0, both, jnp.where(x_lo == 0, own, other))
    theirs = jnp.where(core == 0, both, jnp.where(x_lo == 0, other, own))
    piece = mine + along_x(mine, 2) + along_x(theirs, 1) + along_x(theirs, 3)
    near = [along_y(piece, -k) for k in (2, 1, 3)]
    leaf_r, _, out_l = lax.optimization_barrier((leaf_r, piece, out_l))
    out_r = lax.all_to_all(leaf_r, "blk", split_axis=0, concat_axis=0, tiled=True)
    held = join_first(after(out_l, leaf_r))
    held, near = lax.optimization_barrier((held, near))
    stack = jnp.stack([piece, near[1], near[0], near[2]])
    gathered = [stack] + [to_worker(stack, k) for k in (1, 2, 3)]

    place = jnp.stack([y, z]).astype(jnp.int32)
    members = jnp.where(core == 0, ROWS * N_BLK * N_CUBE, ROWS * N_BLK * N_CUBE // 2).astype(F32).reshape(1)
    found = power(place, members, start_vec.reshape(1, D), gathered)
    found = [found] + [from_worker(found, dz, dc) for dz, dc in ((0, 1), (1, 0), (1, 1))]
    flags = jnp.stack([core, z % 2]).astype(jnp.int32)
    scores = all_scores(flags, found, rows, next_l, next_r)
    return scores, join_second(out_r, held)


def solution(mesh):
    placed_at = (P(("cube", "blk"), None), P(), P(None, ("cube", "blk")), P(("cube", "blk"), None))
    return jax.shard_map(
        per_device,
        mesh=mesh,
        in_specs=placed_at,
        out_specs=(P(None, ("cube", "blk")), P(("cube", "blk"), None)),
        check_vma=False,
    )
```
